128 devices in a mesh: bal: 16 (over z, x), grp: 8 (over y, core).
Axes of the slice: x: 4, y: 4, z: 4, core: 2. Of those that a mesh axis runs over, the one named last changes fastest.
Arguments:
- table: bfloat16 [262144, 512], P(('bal', 'grp')), may hold values from -6 to 6
- item_owner: int32 [8, 4096, 1], P('grp', 'bal'), may hold values from 0 to 127; in each aligned block of 256 rows (0 to 255, 256 to 511, ..., all dimensions but the last counted through in order) at most 8 rows name the same one
- item_row: int32 [8, 4096], P('grp', 'bal'), may hold values from 0 to 2047
- segment: int32 [8, 4096], P('grp', 'bal'), may hold values from 0 to 7, never falling along the last dimension, each value on 1 to 2048 neighbouring positions
- w_in: bfloat16 [512, 1024], replicated, may hold values from -0.25 to 0.25
- w_out: bfloat16 [256, 512], replicated, may hold values from -0.375 to 0.375
- cotangent: bfloat16 [8, 4096, 512], P('grp', 'bal'), may hold values from -6 to 6
Outputs:
- layer_out: bfloat16 [8, 4096, 512], P('grp', 'bal')
- table_grad: float32 [262144, 512], P(('bal', 'grp'))
- w_in_grad: float32 [512, 1024], replicated
- w_out_grad: float32 [256, 512], replicated
The draws below stay inside these ranges and needn't reach their ends.
Inputs may be any that keep to these rules, and one draw needn't show every extreme that they name: `item_owner`: of the actions of one device at most 8 name the same row block, and in some device exactly 8 do. `segment`: along each group's actions the history number never falls; each history holds 1 to 2048 actions and one holds exactly 2048.
All inputs are finite; a program needn't handle non-finite values.
Results may differ from the reference program's by a relative error of at most 0.0091.
Values may be sent and summed in bfloat16 or wider, within the bound.
A program may use at most 128 MiB of HBM per device.

```python
import math
import jax
import jax.numpy as jnp
import numpy as np
from jax import lax

D = 512
HEADS = 4
DH = 64
TOK_DEV = 256
ROWS_DEV = 2048
HD = 256
GROUP_TOK = 4096
LEN_MAX = 2048
SEQ_GRP = 8
CAP = 8
ITEMS = 262144
N_BAL = 16
N_GRP = 8
DEVICES = 128


def touch_ends(result, rng, least, largest):
    spot = [jax.random.randint(jax.random.fold_in(rng, axis), (), 0, length) for axis, length in enumerate(result.shape)]
    longest = result.shape.index(max(result.shape))
    beside = spot[:longest] + [(spot[longest] + 1) % result.shape[longest]] + spot[longest + 1:]
    return result.at[tuple(spot)].set(least).at[tuple(beside)].set(largest)


def level_of(key, dims, shards, smallest, high):
    gain, own = 1.0, jax.random.fold_in(key, 6)
    for dim, blocks in shards:
        steps = jnp.exp(jax.random.uniform(jax.random.fold_in(own, dim), (blocks,), jnp.float32, smallest / len(shards), high / len(shards)))
        gain = gain * jnp.repeat(steps, dims[dim] // blocks).reshape([-1 if axis == dim else 1 for axis in range(len(dims))])
    return gain


def split_up(number_of, total, bound, lean):
    loads = [(1 << 20) // math.isqrt(grade ** lean) + 1 for grade in range(2, number_of + 1)]
    surplus, counts = total - bound - (number_of - 1), [1] * (number_of - 1)
    while surplus > 0:
        free = [i for i in range(number_of - 1) if counts[i] < bound]
        mass, budget = sum([loads[i] for i in free]), surplus
        for i in free:
            more = min(bound - counts[i], max(1, budget * loads[i] // mass), surplus)
            counts[i] = counts[i] + more
            surplus = surplus - more
    return np.array([bound] + counts)


def ragged_sizes(stream_key, count, total, limit, skew):
    if count == 2:
        one = jax.random.randint(stream_key, (), max(1, total - limit), min(limit, total - 1) + 1)
        return jnp.stack([one, total - one])
    lengths = jnp.asarray(split_up(count, total, limit, skew), jnp.int32)
    pairs = (count - 1) // 2
    giver, receiver = lengths[1:1 + 2 * pairs:2], lengths[2:2 + 2 * pairs:2]
    slack = jnp.minimum(giver - 1, limit - receiver)
    moved = jax.random.randint(jax.random.fold_in(stream_key, 1), (pairs,), 0, 1 << 20) % (slack + 1)
    lengths = lengths.at[1:1 + 2 * pairs:2].set(giver - moved).at[2:2 + 2 * pairs:2].set(receiver + moved)
    return lengths[jax.random.permutation(jax.random.fold_in(stream_key, 2), count)]


def deal_out(stream_key, own, number, rows, count, top, limit, skew):
    sequence = jax.random.permutation(stream_key, count)
    heavy_load, common = load_shares(count, rows * top, limit, skew, True), load_shares(count, rows * top, limit, skew, False)
    places = jnp.arange(count)

    def named(lengths, turn):
        used = int((lengths > 0).sum())
        fixed = max(1, used // 4)
        passed = fixed + (places - fixed + turn * (used - fixed)) % max(1, count - fixed)
        return jnp.zeros((count,), jnp.int32).at[sequence[jnp.where(places < fixed, places, passed)]].set(jnp.asarray(lengths, jnp.int32))

    lengths = jnp.where(number % 4 == 0, named(heavy_load, number // 4), named(common, number - number // 4 - 1))
    mixed = jax.random.permutation(jax.random.fold_in(own, 3), count)
    source_of, receiver = mixed[0:count // 2 * 2:2], mixed[1:count // 2 * 2:2]
    room = jnp.minimum(lengths[source_of] - 1, limit - lengths[receiver]) // 2
    room = jnp.where((source_of == sequence[0]) | (receiver == sequence[0]) | (lengths[receiver] == 0), 0, jnp.maximum(room, 0))
    passed = jax.random.randint(jax.random.fold_in(own, 4), (count // 2,), 0, 1 << 20) % (room + 1)
    lengths = lengths.at[source_of].add(-passed).at[receiver].add(passed)
    labels = jnp.searchsorted(jnp.cumsum(lengths), jnp.arange(rows * top), side="right").astype(jnp.int32)
    table = labels.reshape(top, rows).T
    table = table[jax.random.permutation(jax.random.fold_in(own, 1), rows)]
    turn = jax.random.randint(jax.random.fold_in(own, 2), (rows, 1), 0, top)
    return jnp.take_along_axis(table, (jnp.arange(top)[None, :] + turn) % top, axis=1)


def load_shares(count, total, reach, skew, full):
    loads = [(1 << 20) // math.isqrt(standing ** skew) + 1 for standing in range(1, count + 1)]
    largest = reach if full else min(reach, max(-(-total // count), total * loads[0] // sum(loads)))
    least = 1 if total - largest >= count - 1 else 0
    holding, surplus = [largest] + [least] * (count - 1), total - largest - least * (count - 1)
    while surplus > 0:
        movable = [i for i in range(1, count) if holding[i] < largest] or [i for i in range(1, count) if holding[i] < reach]
        whole, budget = sum([loads[i] for i in movable]), surplus
        for i in movable:
            more = min(reach - holding[i], max(1, budget * loads[i] // whole), surplus)
            holding[i] = holding[i] + more
            surplus = surplus - more
    return np.array(holding)


def bell_draw(own_key, extent, scale, limit, split=(), kind=jnp.bfloat16):
    entries = jax.random.normal(own_key, extent, jnp.float32) * scale
    if len(split) > 0:
        entries = level_of(own_key, extent, split, -0.22, 0.18) * entries
    return jnp.clip(entries, min=-limit, max=limit).astype(kind)


def setup_inputs(seed: int = 0) -> dict:
    key_of = jax.random.split(jax.random.key(seed), 8)
    table = bell_draw(key_of[0], (ITEMS, D), 1.0, 6.0, ((0, 128),))
    item_owner_keys = jax.random.split(jax.random.fold_in(key_of[1], 1), N_GRP * GROUP_TOK // TOK_DEV)
    item_owner_turns = jax.random.permutation(jax.random.fold_in(key_of[1], 3), N_GRP * GROUP_TOK // TOK_DEV)
    item_owner = jax.vmap(lambda own, number: deal_out(jax.random.fold_in(key_of[1], 2), own, number, TOK_DEV, DEVICES, 1, CAP, 2))(item_owner_keys, item_owner_turns).reshape((N_GRP, GROUP_TOK, 1))
    item_row = touch_ends(jax.random.randint(key_of[2], (N_GRP, GROUP_TOK), 0, ROWS_DEV), jax.random.fold_in(key_of[2], 1), 0, ROWS_DEV - 1).astype(jnp.int32)
    segment = jax.vmap(lambda own: jnp.searchsorted(jnp.cumsum(ragged_sizes(own, SEQ_GRP, GROUP_TOK, LEN_MAX, 2)), jnp.arange(GROUP_TOK), side="right"))(jax.random.split(key_of[3], N_GRP)).reshape((N_GRP, GROUP_TOK)).astype(jnp.int32)
    w_in = bell_draw(key_of[4], (D, 4 * HD), D ** -0.5, 0.25)
    w_out = bell_draw(key_of[5], (HD, D), HD ** -0.5, 0.375)
    cotangent = bell_draw(key_of[6], (N_GRP, GROUP_TOK, D), 1.0, 6.0, ((0, 8), (1, 16)))
    return dict(table=table, item_owner=item_owner, item_row=item_row, segment=segment, w_in=w_in, w_out=w_out, cotangent=cotangent)


norm_eps = 1e-06
contract_rows = (((0,), (0,)), ((), ()))
contract_cols = (((1,), (1,)), ((), ()))

def layer_norm(values):
    average = lax.optimization_barrier(jnp.mean(values, axis=-1, keepdims=True))
    centred = values - average
    spread = lax.optimization_barrier(jnp.mean(centred * centred, axis=-1, keepdims=True))
    return centred * lax.rsqrt(spread + norm_eps)

def output_norm(attended, gate):
    return layer_norm(attended) * gate

def silu_slope(values):
    sigmoids = jax.nn.sigmoid(values)
    return sigmoids * (1.0 + values * (1.0 - sigmoids))

def rounded(values):
    return lax.optimization_barrier(values.astype(jnp.bfloat16)).astype(jnp.float32)

def by_heads(values):
    return values.astype(jnp.float32).reshape(values.shape[0], HEADS, DH)

def visible_pairs(query_pos, query_seg, key_pos, key_seg):
    return (query_seg[:, None] == key_seg[None, :]) & (key_pos[None, :] <= query_pos[:, None])

def pair_terms(queries, keys_in, visible):
    scores = jnp.einsum('qhd,khd->hqk', queries, keys_in)
    sigmoids = jax.nn.sigmoid(scores)
    weight = jnp.where(visible[None], scores * sigmoids / LEN_MAX, 0.0)
    slopes = jnp.where(visible[None], sigmoids * (1.0 + scores * (1.0 - sigmoids)) / LEN_MAX, 0.0)
    return (weight, slopes)

def group_forward(operands):
    queries, keys_in, values_in, segments = operands
    positions = jnp.arange(GROUP_TOK, dtype=jnp.int32)
    key_heads = by_heads(keys_in)
    value_heads = by_heads(values_in)

    def query_block(block):
        query_part, pos_part, seg_part = block
        weight, _ = pair_terms(by_heads(query_part), key_heads, visible_pairs(pos_part, seg_part, positions, segments))
        return jnp.einsum('hqk,khd->qhd', rounded(weight), value_heads).reshape(TOK_DEV, HD)
    blocks = (queries.reshape(N_BAL, TOK_DEV, HD), positions.reshape(N_BAL, TOK_DEV), segments.reshape(N_BAL, TOK_DEV))
    return lax.map(query_block, blocks).reshape(GROUP_TOK, HD)

def group_backward(operands):
    queries, keys_in, values_in, deltas, segments = operands
    positions = jnp.arange(GROUP_TOK, dtype=jnp.int32)
    query_heads = by_heads(queries)
    key_heads = by_heads(keys_in)
    value_heads = by_heads(values_in)
    delta_heads = by_heads(deltas)

    def query_block(block):
        query_part, delta_part, pos_part, seg_part = block
        weight, slopes = pair_terms(by_heads(query_part), key_heads, visible_pairs(pos_part, seg_part, positions, segments))
        product = jnp.einsum('qhd,khd->hqk', by_heads(delta_part), value_heads)
        d_score = rounded(product * slopes)
        return jnp.einsum('hqk,khd->qhd', d_score, key_heads).reshape(TOK_DEV, HD).astype(jnp.bfloat16)

    def key_block(block):
        key_part, value_part, pos_part, seg_part = block
        weight, slopes = pair_terms(query_heads, by_heads(key_part), visible_pairs(positions, segments, pos_part, seg_part))
        product = jnp.einsum('qhd,khd->hqk', delta_heads, by_heads(value_part))
        d_score = rounded(product * slopes)
        key_grad = jnp.einsum('hqk,qhd->khd', d_score, query_heads).reshape(TOK_DEV, HD).astype(jnp.bfloat16)
        value_grad = jnp.einsum('hqk,qhd->khd', rounded(weight), delta_heads).reshape(TOK_DEV, HD).astype(jnp.bfloat16)
        return (key_grad, value_grad)
    pos_blocks = positions.reshape(N_BAL, TOK_DEV)
    seg_blocks = segments.reshape(N_BAL, TOK_DEV)
    query_grad = lax.map(query_block, (queries.reshape(N_BAL, TOK_DEV, HD), deltas.reshape(N_BAL, TOK_DEV, HD), pos_blocks, seg_blocks))
    key_grad, value_grad = lax.map(key_block, (keys_in.reshape(N_BAL, TOK_DEV, HD), values_in.reshape(N_BAL, TOK_DEV, HD), pos_blocks, seg_blocks))
    return (query_grad.reshape(GROUP_TOK, HD), key_grad.reshape(GROUP_TOK, HD), value_grad.reshape(GROUP_TOK, HD))

def groups(values):
    return values.reshape(N_GRP, GROUP_TOK, HD)

def reference(table, item_owner, item_row, segment, w_in, w_out, cotangent):
    index = (item_owner[:, :, 0] * ROWS_DEV + item_row).reshape(-1).astype(jnp.int32)
    embedded = table[index]
    normed = layer_norm(embedded.astype(jnp.float32)).astype(jnp.bfloat16)
    pre_act = jnp.dot(normed, w_in, preferred_element_type=jnp.float32)
    activated = jax.nn.silu(pre_act)
    gate = activated[:, :HD].astype(jnp.bfloat16)
    value_rows = activated[:, HD:2 * HD].astype(jnp.bfloat16)
    query_rows = activated[:, 2 * HD:3 * HD].astype(jnp.bfloat16)
    key_rows = activated[:, 3 * HD:].astype(jnp.bfloat16)
    attended = lax.map(group_forward, (groups(query_rows), groups(key_rows), groups(value_rows), segment)).reshape(-1, HD)
    mixed, post_back = jax.vjp(output_norm, attended, gate.astype(jnp.float32))
    mixed_low = mixed.astype(jnp.bfloat16)
    layer_out = (jnp.dot(mixed_low, w_out, preferred_element_type=jnp.float32) + embedded.astype(jnp.float32)).astype(jnp.bfloat16)
    upstream = cotangent.reshape(-1, D)
    w_out_grad = lax.dot_general(mixed_low, upstream, contract_rows, preferred_element_type=jnp.float32)
    d_mixed = lax.dot_general(upstream, w_out, contract_cols, preferred_element_type=jnp.float32)
    d_attended, d_gate = post_back(d_mixed)
    deltas = d_attended.astype(jnp.bfloat16)
    gate_grad = d_gate.astype(jnp.bfloat16)
    query_grad, key_grad, value_grad = lax.map(group_backward, (groups(query_rows), groups(key_rows), groups(value_rows), groups(deltas), segment))
    joined = jnp.concatenate([gate_grad, value_grad.reshape(-1, HD), query_grad.reshape(-1, HD), key_grad.reshape(-1, HD)], axis=1)
    d_pre = (joined.astype(jnp.float32) * silu_slope(pre_act)).astype(jnp.bfloat16)
    w_in_grad = lax.dot_general(normed, d_pre, contract_rows, preferred_element_type=jnp.float32)
    d_normed = lax.dot_general(d_pre, w_in, contract_cols, preferred_element_type=jnp.float32)
    _, norm_back = jax.vjp(layer_norm, embedded.astype(jnp.float32))
    d_embedded = norm_back(d_normed)[0] + upstream.astype(jnp.float32)
    table_grad = jnp.zeros((ITEMS, D), jnp.float32).at[index].add(d_embedded)
    return (layer_out.reshape(N_GRP, GROUP_TOK, D), table_grad, w_in_grad, w_out_grad)
```

```python
import jax
import jax.numpy as jnp
from jax import lax
from jax.experimental import pallas as pl
from jax.experimental.pallas import tpu as pltpu
from jax.sharding import PartitionSpec as P

HEADS = 4
DH = 64


norm_eps = 1e-06
contract_rows = (((0,), (0,)), ((), ()))
contract_cols = (((1,), (1,)), ((), ()))


def layer_norm(values):
    average = jnp.mean(values, axis=-1, keepdims=True)
    centred = values - average
    spread = jnp.mean(centred * centred, axis=-1, keepdims=True)
    return centred * lax.rsqrt(spread + norm_eps)


def output_norm(attended, gate):
    return layer_norm(attended) * gate


def silu_slope(values):
    sigmoids = jax.nn.sigmoid(values)
    return sigmoids * (1.0 + values * (1.0 - sigmoids))


def by_heads(values):
    return values.reshape(values.shape[0], HEADS, DH)


def visible_pairs(query_pos, query_seg, key_pos, key_seg):
    return (query_seg[:, None] == key_seg[None, :]) & (key_pos[None, :] <= query_pos[:, None])


def pair_terms(queries, keys_in, visible, len_max):
    scores = jnp.einsum("qhd,khd->hqk", queries, keys_in, preferred_element_type=jnp.float32)
    sigmoids = jax.nn.sigmoid(scores)
    weight = jnp.where(visible[None], scores * sigmoids / len_max, 0.0)
    slopes = jnp.where(visible[None], sigmoids * (1.0 + scores * (1.0 - sigmoids)) / len_max, 0.0)
    return (weight, slopes)


def sweep(block_step, carry, amount):
    block = amount
    while block > 1024 and block % 2 == 0:
        block = block // 2
    return lax.fori_loop(
        0,
        amount // block,
        lambda counter, current: block_step(current, counter * block, block),
        carry,
    )


MESH = pl.DeviceIdType.MESH
BF = jnp.bfloat16
F32 = jnp.float32
TOK = 256
WIDTH = 512
CAP = 8
ROWS = 2048
NB = 16
NG = 8
DEV = NB * NG
SLOTS = DEV * CAP


def iota(shape, dim):
    return lax.broadcasted_iota(jnp.int32, shape, dim)


def hot(mask):
    return jnp.where(mask, 1.0, 0.0).astype(BF)


def dot(a, b):
    return jnp.dot(a, b, preferred_element_type=F32)


def dot_t(a, b):
    return lax.dot_general(a, b, (((1,), (1,)), ((), ())), preferred_element_type=F32)


def column_of(line):
    size = line.shape[1]
    eye = iota((size, size), 0) == iota((size, size), 1)
    return jnp.sum(jnp.where(eye, line, 0.0), axis=1, keepdims=True)


def line_of(column):
    size = column.shape[0]
    eye = iota((size, size), 0) == iota((size, size), 1)
    return jnp.sum(jnp.where(eye, column, 0.0), axis=0, keepdims=True)


def device(p):
    return (p // NG, lax.rem(p, NG))


def greet_all(me):
    barrier = pltpu.get_barrier_semaphore()

    def greet(k, carry):
        pl.semaphore_signal(
            barrier, inc=1, device_id=device(lax.rem(me + k, DEV)), device_id_type=MESH
        )
        return carry

    lax.fori_loop(1, DEV, greet, 0)
    return barrier


def paired_halves(rows):
    count = rows.shape[0] // CAP
    split = rows.reshape(count, CAP, WIDTH)
    joined = jnp.concatenate([split[:, :, : WIDTH // 2], split[:, :, WIDTH // 2 :]], axis=1)
    return joined.reshape(count * 2 * CAP, WIDTH // 2).astype(BF)


def wait_bytes(view, sem):
    pltpu.make_async_copy(view, view, sem).wait()


def fetch_kernel(
    owner_ref, row_ref, seg_ref, table_hbm,
    emb_ref, want_ref, slot_ref, start_ref,
    table_v, asked, asks, want_v, rows_out, rows_in, count_out, count_in,
    sems, count_send, count_recv,
):
    b, g = lax.axis_index("bal"), lax.axis_index("grp")
    me = b * NG + g
    barrier = greet_all(me)
    load = pltpu.make_async_copy(table_hbm, table_v, sems.at[0])
    load.start()
    owner = owner_ref[...]
    owner_f = owner.astype(F32)
    lanes = iota((TOK, 128), 1)
    named = jnp.where(owner == lanes, 1.0, 0.0)
    before = hot(iota((TOK, TOK), 0) > iota((TOK, TOK), 1))
    rank = jnp.sum(dot(before, named.astype(BF)) * named, axis=1, keepdims=True)
    slot = owner_f * CAP + rank
    slot_ref[...] = jnp.broadcast_to(line_of(slot), (8, TOK)).astype(jnp.int32)
    ask = column_of(row_ref[...].astype(F32)) + 1.0
    high = jnp.floor(ask * (1.0 / 64.0))
    low = ask - 64.0 * high
    mine = rank.astype(jnp.int32) == lanes // 16
    named_t = hot(line_of(owner_f).astype(jnp.int32) == iota((DEV, TOK), 0))
    asked[...] = (
        64.0 * dot(named_t, jnp.where(mine, high, 0.0).astype(BF))
        + dot(named_t, jnp.where(mine, low, 0.0).astype(BF))
    ).astype(jnp.int32).reshape(DEV, 1, 128)
    seg = column_of(seg_ref[...].astype(F32)).astype(jnp.int32)
    below = jnp.sum(jnp.where(seg < lanes, 1.0, 0.0), axis=0, keepdims=True)
    count_out[...] = jnp.broadcast_to(below, (8, 128))
    count_in[b] = jnp.broadcast_to(below, (8, 128))
    own = pltpu.make_async_copy(asked.at[me], asks.at[me], sems.at[1])
    own.start()
    own.wait()
    pl.semaphore_wait(barrier, DEV - 1)

    def ask_for(k, carry):
        p = lax.rem(me + k, DEV)
        pltpu.make_async_remote_copy(
            src_ref=asked.at[p], dst_ref=asks.at[me], send_sem=sems.at[2], recv_sem=sems.at[3],
            device_id=device(p), device_id_type=MESH,
        ).start()
        return carry

    lax.fori_loop(1, DEV, ask_for, 0)
    tallies = []
    for k in range(1, NB):
        tally = pltpu.make_async_remote_copy(
            src_ref=count_out, dst_ref=count_in.at[b], send_sem=count_send.at[k],
            recv_sem=count_recv.at[k], device_id=(lax.rem(b + k, NB), g), device_id_type=MESH,
        )
        tally.start()
        tallies.append(tally)
    load.wait()
    wait_bytes(asks.at[pl.ds(0, DEV - 1)], sems.at[3])
    got = asks[...].reshape(DEV, 128).astype(F32)
    got_high = jnp.floor(got * (1.0 / 64.0))
    got_low = got - 64.0 * got_high
    spread = hot(iota((SLOTS, DEV), 0) // CAP == iota((SLOTS, DEV), 1))
    every = 64.0 * dot(spread, got_high.astype(BF)) + dot(spread, got_low.astype(BF))
    pick = lax.rem(iota((SLOTS, 128), 0), CAP) * 16 == iota((SLOTS, 128), 1)
    want = jnp.sum(jnp.where(pick, every, 0.0), axis=1, keepdims=True) - 1.0
    want = jnp.broadcast_to(want, (SLOTS, 128))
    want_v[...] = want.astype(jnp.int32)
    want_ref[...] = want.T[:8].astype(jnp.int32)
    part = SLOTS // 4
    peers = DEV // 4

    def serve(i, carry):
        c = lax.rem(me // peers + i, 4)
        rows = want_v[pl.ds(pl.multiple_of(c * part, part), part), :]
        chosen = hot(rows[:, :1] == iota((part, ROWS), 1))
        found = paired_halves(dot(chosen, table_v[...]))
        rows_out[pl.ds(pl.multiple_of(c * 2 * part, 2 * part), 2 * part), :] = found

        def give(k, inner):
            p = c * peers + lax.rem(me + k, peers)

            @pl.when(p != me)
            def _():
                pltpu.make_async_remote_copy(
                    src_ref=rows_out.at[pl.ds(pl.multiple_of(p * 16, 16), 16)],
                    dst_ref=rows_in.at[pl.ds(pl.multiple_of(me * 16, 16), 16)],
                    send_sem=sems.at[4], recv_sem=sems.at[5],
                    device_id=device(p), device_id_type=MESH,
                ).start()

            return inner

        return lax.fori_loop(0, peers, give, carry)

    lax.fori_loop(0, 4, serve, 0)
    home = pl.ds(pl.multiple_of(me * 16, 16), 16)
    own = pltpu.make_async_copy(rows_out.at[home], rows_in.at[home], sems.at[1])
    own.start()
    for tally in tallies:
        tally.wait()
    total = jnp.sum(count_in[...], axis=0)
    start_ref[...] = total.astype(jnp.int32)
    place = (slot.astype(jnp.int32) // CAP) * 16 + lax.rem(slot.astype(jnp.int32), CAP)
    spots = iota((TOK, 2 * SLOTS), 1)
    left, right = hot(place == spots), hot(place + CAP == spots)
    own.wait()
    wait_bytes(rows_in.at[pl.ds(0, 16 * (DEV - 1))], sems.at[5])
    emb_ref[:, : WIDTH // 2] = dot(left, rows_in[...]).astype(BF)
    emb_ref[:, WIDTH // 2 :] = dot(right, rows_in[...]).astype(BF)
    wait_bytes(asked.at[pl.ds(0, DEV - 1)], sems.at[2])
    wait_bytes(rows_out.at[pl.ds(0, 16 * (DEV - 1))], sems.at[4])


VMEM = pl.BlockSpec(memory_space=pltpu.VMEM)
ANY = pl.BlockSpec(memory_space=pl.ANY)


def fetch(owner, row, seg, table):
    return pl.pallas_call(
        fetch_kernel,
        out_shape=(
            jax.ShapeDtypeStruct((TOK, WIDTH), BF),
            jax.ShapeDtypeStruct((8, SLOTS), jnp.int32),
            jax.ShapeDtypeStruct((8, TOK), jnp.int32),
            jax.ShapeDtypeStruct((8, 128), jnp.int32),
        ),
        in_specs=[VMEM, VMEM, VMEM, ANY],
        out_specs=(VMEM, VMEM, VMEM, VMEM),
        scratch_shapes=[
            pltpu.VMEM((ROWS, WIDTH), BF),
            pltpu.VMEM((DEV, 1, 128), jnp.int32),
            pltpu.VMEM((DEV, 1, 128), jnp.int32),
            pltpu.VMEM((SLOTS, 128), jnp.int32),
            pltpu.VMEM((2 * SLOTS, WIDTH // 2), BF),
            pltpu.VMEM((2 * SLOTS, WIDTH // 2), BF),
            pltpu.VMEM((8, 128), F32),
            pltpu.VMEM((NB, 8, 128), F32),
            pltpu.SemaphoreType.DMA((6,)),
            pltpu.SemaphoreType.DMA((NB,)),
            pltpu.SemaphoreType.DMA((NB,)),
        ],
        compiler_params=pltpu.CompilerParams(
            collective_id=0, has_side_effects=True, vmem_limit_bytes=48 << 20
        ),
        name="fetch_rows",
    )(owner, row, seg, table)


def return_kernel(slot_ref, grad_ref, landed_ref, out_v, in_v, sems):
    b, g = lax.axis_index("bal"), lax.axis_index("grp")
    me = b * NG + g
    barrier = greet_all(me)
    part = SLOTS // 4
    peers = DEV // 4
    pl.semaphore_wait(barrier, DEV - 1)

    def serve(i, carry):
        c = lax.rem(me // peers + i, 4)
        chosen = hot(slot_ref[:1, :] == iota((part, TOK), 0) + c * part)
        found = paired_halves(dot(chosen, grad_ref[...]))
        out_v[pl.ds(pl.multiple_of(c * 2 * part, 2 * part), 2 * part), :] = found

        def give(k, inner):
            p = c * peers + lax.rem(me + k, peers)

            @pl.when(p != me)
            def _():
                pltpu.make_async_remote_copy(
                    src_ref=out_v.at[pl.ds(pl.multiple_of(p * 16, 16), 16)],
                    dst_ref=in_v.at[pl.ds(pl.multiple_of(me * 16, 16), 16)],
                    send_sem=sems.at[0], recv_sem=sems.at[1],
                    device_id=device(p), device_id_type=MESH,
                ).start()

            return inner

        return lax.fori_loop(0, peers, give, carry)

    lax.fori_loop(0, 4, serve, 0)
    home = pl.ds(pl.multiple_of(me * 16, 16), 16)
    own = pltpu.make_async_copy(out_v.at[home], in_v.at[home], sems.at[2])
    own.start()
    own.wait()
    wait_bytes(in_v.at[pl.ds(0, 16 * (DEV - 1))], sems.at[1])
    halves = in_v[...].astype(F32).reshape(DEV, 2 * CAP, WIDTH // 2)
    whole = jnp.concatenate([halves[:, :CAP], halves[:, CAP:]], axis=2)
    landed_ref[...] = whole.reshape(SLOTS, WIDTH).astype(BF)
    wait_bytes(out_v.at[pl.ds(0, 16 * (DEV - 1))], sems.at[0])


def give_back(slot, grad):
    return pl.pallas_call(
        return_kernel,
        out_shape=jax.ShapeDtypeStruct((SLOTS, WIDTH), BF),
        in_specs=[VMEM, VMEM],
        out_specs=VMEM,
        scratch_shapes=[
            pltpu.VMEM((2 * SLOTS, WIDTH // 2), BF),
            pltpu.VMEM((2 * SLOTS, WIDTH // 2), BF),
            pltpu.SemaphoreType.DMA((3,)),
        ],
        compiler_params=pltpu.CompilerParams(
            collective_id=1, has_side_effects=True, vmem_limit_bytes=48 << 20
        ),
        name="return_grads",
    )(slot, grad)


def scatter_kernel(want_ref, landed_ref, out_ref):
    part = out_ref.shape[0]
    rows = iota((part, SLOTS), 0) + pl.program_id(0) * part
    out_ref[...] = dot(hot(want_ref[:1, :] == rows), landed_ref[...])


def scatter_add(want, landed):
    part = 256
    return pl.pallas_call(
        scatter_kernel,
        grid=(ROWS // part,),
        out_shape=jax.ShapeDtypeStruct((ROWS, WIDTH), F32),
        in_specs=[
            pl.BlockSpec((8, SLOTS), lambda i: (0, 0)),
            pl.BlockSpec((SLOTS, WIDTH), lambda i: (0, 0)),
        ],
        out_specs=pl.BlockSpec((part, WIDTH), lambda i: (i, 0)),
        compiler_params=pltpu.CompilerParams(vmem_limit_bytes=32 << 20),
        name="scatter_rows",
    )(want, landed)


def per_device(table, item_owner, item_row, segment, w_in, w_out, cotangent):
    n_bal = lax.axis_size("bal")
    rows_here = item_row[0]
    segments = segment[0]
    upstream = cotangent[0]
    actions = rows_here.shape[0]
    hidden = w_out.shape[0]
    group_len = actions * n_bal
    len_max = group_len // 2
    embedded, want, slot, _ = fetch(item_owner[0], item_row, segment, table)
    normed = layer_norm(embedded.astype(jnp.float32)).astype(jnp.bfloat16)
    pre_act = jnp.dot(normed, w_in, preferred_element_type=jnp.float32)
    activated = jax.nn.silu(pre_act)
    gate = activated[:, :hidden].astype(jnp.bfloat16)
    value_rows = activated[:, hidden : 2 * hidden].astype(jnp.bfloat16)
    query_rows = activated[:, 2 * hidden : 3 * hidden].astype(jnp.bfloat16)
    key_rows = activated[:, 3 * hidden :].astype(jnp.bfloat16)
    all_segments = lax.all_gather(segments, "bal", axis=0, tiled=True)
    my_pos = lax.axis_index("bal") * actions + jnp.arange(actions, dtype=jnp.int32)
    query_heads = by_heads(query_rows)
    head_zeros = jnp.zeros((actions, HEADS, DH), jnp.float32)
    key_part = lax.all_gather(key_rows, "bal", axis=0, tiled=True)
    value_part = lax.all_gather(value_rows, "bal", axis=0, tiled=True)

    def block_step(running, offset, amount):
        key_block = by_heads(lax.dynamic_slice_in_dim(key_part, offset, amount, 0))
        value_block = by_heads(lax.dynamic_slice_in_dim(value_part, offset, amount, 0))
        key_pos = offset + jnp.arange(amount, dtype=jnp.int32)
        key_seg = lax.dynamic_slice_in_dim(all_segments, offset, amount, 0)
        weight, _ = pair_terms(
            query_heads, key_block, visible_pairs(my_pos, segments, key_pos, key_seg), len_max
        )
        return running + jnp.einsum(
            "hqk,khd->qhd",
            weight.astype(jnp.bfloat16),
            value_block,
            preferred_element_type=jnp.float32,
        )

    attended = sweep(block_step, head_zeros, key_part.shape[0]).reshape(actions, hidden)
    mixed, post_back = jax.vjp(output_norm, attended, gate.astype(jnp.float32))
    mixed_low = mixed.astype(jnp.bfloat16)
    layer_out = (
        jnp.dot(mixed_low, w_out, preferred_element_type=jnp.float32) + embedded.astype(jnp.float32)
    ).astype(jnp.bfloat16)
    w_out_part = lax.dot_general(
        mixed_low, upstream, contract_rows, preferred_element_type=jnp.float32
    )
    d_mixed = lax.dot_general(upstream, w_out, contract_cols, preferred_element_type=jnp.float32)
    d_attended, d_gate = post_back(d_mixed)
    deltas = d_attended.astype(jnp.bfloat16)
    gate_grad = d_gate.astype(jnp.bfloat16)
    delta_heads = by_heads(deltas)
    group_zeros = jnp.zeros((group_len, hidden), jnp.float32)
    joint_key_part = lax.all_gather(key_rows, "bal", axis=0, tiled=True)
    joint_value_part = lax.all_gather(value_rows, "bal", axis=0, tiled=True)

    def block_step(running, offset, amount):
        query_total, key_terms, value_terms = running
        key_block = by_heads(lax.dynamic_slice_in_dim(joint_key_part, offset, amount, 0))
        value_block = by_heads(lax.dynamic_slice_in_dim(joint_value_part, offset, amount, 0))
        key_pos = offset + jnp.arange(amount, dtype=jnp.int32)
        key_seg = lax.dynamic_slice_in_dim(all_segments, offset, amount, 0)
        weight, slopes = pair_terms(
            query_heads, key_block, visible_pairs(my_pos, segments, key_pos, key_seg), len_max
        )
        product = jnp.einsum(
            "qhd,khd->hqk", delta_heads, value_block, preferred_element_type=jnp.float32
        )
        d_score = (product * slopes).astype(jnp.bfloat16)
        query_total = query_total + jnp.einsum(
            "hqk,khd->qhd", d_score, key_block, preferred_element_type=jnp.float32
        )
        key_piece_grad = jnp.einsum(
            "hqk,qhd->khd", d_score, query_heads, preferred_element_type=jnp.float32
        )
        value_piece_grad = jnp.einsum(
            "hqk,qhd->khd",
            weight.astype(jnp.bfloat16),
            delta_heads,
            preferred_element_type=jnp.float32,
        )
        key_terms = lax.dynamic_update_slice_in_dim(
            key_terms, key_piece_grad.reshape(amount, hidden), offset, 0
        )
        value_terms = lax.dynamic_update_slice_in_dim(
            value_terms, value_piece_grad.reshape(amount, hidden), offset, 0
        )
        return (query_total, key_terms, value_terms)

    query_grad, key_terms, value_terms = sweep(
        block_step, (head_zeros, group_zeros, group_zeros), joint_key_part.shape[0]
    )
    key_grad, value_grad = (
        lax.psum_scatter(key_terms, "bal", scatter_dimension=0, tiled=True),
        lax.psum_scatter(value_terms, "bal", scatter_dimension=0, tiled=True),
    )
    joined = jnp.concatenate(
        [
            gate_grad,
            value_grad.astype(jnp.bfloat16),
            query_grad.reshape(actions, hidden).astype(jnp.bfloat16),
            key_grad.astype(jnp.bfloat16),
        ],
        axis=1,
    )
    d_pre = (joined.astype(jnp.float32) * silu_slope(pre_act)).astype(jnp.bfloat16)
    w_in_part = lax.dot_general(normed, d_pre, contract_rows, preferred_element_type=jnp.float32)
    d_normed = lax.dot_general(d_pre, w_in, contract_cols, preferred_element_type=jnp.float32)
    _, norm_back = jax.vjp(layer_norm, embedded.astype(jnp.float32))
    d_embedded = norm_back(d_normed)[0] + upstream.astype(jnp.float32)
    landed = give_back(slot, d_embedded.astype(BF))
    table_grad = scatter_add(want, landed)
    w_in_grad, w_out_grad = lax.psum((w_in_part, w_out_part), ("bal", "grp"))
    return (layer_out[None], table_grad, w_in_grad, w_out_grad)


def solution(mesh):
    placed = (
        P(("bal", "grp"), None),
        P("grp", "bal", None),
        P("grp", "bal"),
        P("grp", "bal"),
        P(),
        P(),
        P("grp", "bal", None),
    )
    return jax.shard_map(
        per_device,
        mesh=mesh,
        in_specs=placed,
        out_specs=(P("grp", "bal", None), P(("bal", "grp"), None), P(), P()),
        check_vma=False,
    )
```

```python
import jax
import jax.numpy as jnp
from jax import lax
from jax.experimental import pallas as pl
from jax.experimental.pallas import tpu as pltpu
from jax.sharding import PartitionSpec as P

MESH = pl.DeviceIdType.MESH
BF = jnp.bfloat16
F32 = jnp.float32
TOK = 256
WIDTH = 512
CAP = 8
ROWS = 2048
NB = 16
NG = 8
DEV = NB * NG
SLOTS = DEV * CAP


def iota(shape, dim):
    return lax.broadcasted_iota(jnp.int32, shape, dim)


def hot(mask):
    return jnp.where(mask, 1.0, 0.0).astype(BF)


def dot(a, b):
    return jnp.dot(a, b, preferred_element_type=F32)


def dot_t(a, b):
    return lax.dot_general(a, b, (((1,), (1,)), ((), ())), preferred_element_type=F32)


def column_of(line):
    size = line.shape[1]
    eye = iota((size, size), 0) == iota((size, size), 1)
    return jnp.sum(jnp.where(eye, line, 0.0), axis=1, keepdims=True)


def line_of(column):
    size = column.shape[0]
    eye = iota((size, size), 0) == iota((size, size), 1)
    return jnp.sum(jnp.where(eye, column, 0.0), axis=0, keepdims=True)


def device(p):
    return (p // NG, lax.rem(p, NG))


def greet_all(me):
    barrier = pltpu.get_barrier_semaphore()

    def greet(k, carry):
        pl.semaphore_signal(
            barrier, inc=1, device_id=device(lax.rem(me + k, DEV)), device_id_type=MESH
        )
        return carry

    lax.fori_loop(1, DEV, greet, 0)
    return barrier


def paired_halves(rows):
    count = rows.shape[0] // CAP
    split = rows.reshape(count, CAP, WIDTH)
    joined = jnp.concatenate([split[:, :, : WIDTH // 2], split[:, :, WIDTH // 2 :]], axis=1)
    return joined.reshape(count * 2 * CAP, WIDTH // 2).astype(BF)


def wait_bytes(view, sem):
    pltpu.make_async_copy(view, view, sem).wait()


def fetch_kernel(
    owner_ref, row_ref, seg_ref, table_hbm,
    emb_ref, want_ref, slot_ref, start_ref,
    table_v, asked, asks, want_v, rows_out, rows_in, count_out, count_in,
    sems, count_send, count_recv,
):
    b, g = lax.axis_index("bal"), lax.axis_index("grp")
    me = b * NG + g
    barrier = greet_all(me)
    load = pltpu.make_async_copy(table_hbm, table_v, sems.at[0])
    load.start()
    owner = owner_ref[...]
    owner_f = owner.astype(F32)
    lanes = iota((TOK, 128), 1)
    named = jnp.where(owner == lanes, 1.0, 0.0)
    before = hot(iota((TOK, TOK), 0) > iota((TOK, TOK), 1))
    rank = jnp.sum(dot(before, named.astype(BF)) * named, axis=1, keepdims=True)
    slot = owner_f * CAP + rank
    slot_ref[...] = jnp.broadcast_to(line_of(slot), (8, TOK)).astype(jnp.int32)
    ask = column_of(row_ref[...].astype(F32)) + 1.0
    high = jnp.floor(ask * (1.0 / 64.0))
    low = ask - 64.0 * high
    mine = rank.astype(jnp.int32) == lanes // 16
    named_t = hot(line_of(owner_f).astype(jnp.int32) == iota((DEV, TOK), 0))
    asked[...] = (
        64.0 * dot(named_t, jnp.where(mine, high, 0.0).astype(BF))
        + dot(named_t, jnp.where(mine, low, 0.0).astype(BF))
    ).astype(jnp.int32).reshape(DEV, 1, 128)
    seg = column_of(seg_ref[...].astype(F32)).astype(jnp.int32)
    below = jnp.sum(jnp.where(seg < lanes, 1.0, 0.0), axis=0, keepdims=True)
    count_out[...] = jnp.broadcast_to(below, (8, 128))
    count_in[b] = jnp.broadcast_to(below, (8, 128))
    own = pltpu.make_async_copy(asked.at[me], asks.at[me], sems.at[1])
    own.start()
    own.wait()
    pl.semaphore_wait(barrier, DEV - 1)

    def ask_for(k, carry):
        p = lax.rem(me + k, DEV)
        pltpu.make_async_remote_copy(
            src_ref=asked.at[p], dst_ref=asks.at[me], send_sem=sems.at[2], recv_sem=sems.at[3],
            device_id=device(p), device_id_type=MESH,
        ).start()
        return carry

    lax.fori_loop(1, DEV, ask_for, 0)
    tallies = []
    for k in range(1, NB):
        tally = pltpu.make_async_remote_copy(
            src_ref=count_out, dst_ref=count_in.at[b], send_sem=count_send.at[k],
            recv_sem=count_recv.at[k], device_id=(lax.rem(b + k, NB), g), device_id_type=MESH,
        )
        tally.start()
        tallies.append(tally)
    load.wait()
    wait_bytes(asks.at[pl.ds(0, DEV - 1)], sems.at[3])
    got = asks[...].reshape(DEV, 128).astype(F32)
    got_high = jnp.floor(got * (1.0 / 64.0))
    got_low = got - 64.0 * got_high
    spread = hot(iota((SLOTS, DEV), 0) // CAP == iota((SLOTS, DEV), 1))
    every = 64.0 * dot(spread, got_high.astype(BF)) + dot(spread, got_low.astype(BF))
    pick = lax.rem(iota((SLOTS, 128), 0), CAP) * 16 == iota((SLOTS, 128), 1)
    want = jnp.sum(jnp.where(pick, every, 0.0), axis=1, keepdims=True) - 1.0
    want = jnp.broadcast_to(want, (SLOTS, 128))
    want_v[...] = want.astype(jnp.int32)
    want_ref[...] = want.T[:8].astype(jnp.int32)
    part = SLOTS // 4
    peers = DEV // 4

    def serve(i, carry):
        c = lax.rem(me // peers + i, 4)
        rows = want_v[pl.ds(pl.multiple_of(c * part, part), part), :]
        chosen = hot(rows[:, :1] == iota((part, ROWS), 1))
        found = paired_halves(dot(chosen, table_v[...]))
        rows_out[pl.ds(pl.multiple_of(c * 2 * part, 2 * part), 2 * part), :] = found

        def give(k, inner):
            p = c * peers + lax.rem(me + k, peers)

            @pl.when(p != me)
            def _():
                pltpu.make_async_remote_copy(
                    src_ref=rows_out.at[pl.ds(pl.multiple_of(p * 16, 16), 16)],
                    dst_ref=rows_in.at[pl.ds(pl.multiple_of(me * 16, 16), 16)],
                    send_sem=sems.at[4], recv_sem=sems.at[5],
                    device_id=device(p), device_id_type=MESH,
                ).start()

            return inner

        return lax.fori_loop(0, peers, give, carry)

    lax.fori_loop(0, 4, serve, 0)
    home = pl.ds(pl.multiple_of(me * 16, 16), 16)
    own = pltpu.make_async_copy(rows_out.at[home], rows_in.at[home], sems.at[1])
    own.start()
    for tally in tallies:
        tally.wait()
    total = jnp.sum(count_in[...], axis=0)
    start_ref[...] = total.astype(jnp.int32)
    place = (slot.astype(jnp.int32) // CAP) * 16 + lax.rem(slot.astype(jnp.int32), CAP)
    spots = iota((TOK, 2 * SLOTS), 1)
    left, right = hot(place == spots), hot(place + CAP == spots)
    own.wait()
    wait_bytes(rows_in.at[pl.ds(0, 16 * (DEV - 1))], sems.at[5])
    emb_ref[:, : WIDTH // 2] = dot(left, rows_in[...]).astype(BF)
    emb_ref[:, WIDTH // 2 :] = dot(right, rows_in[...]).astype(BF)
    wait_bytes(asked.at[pl.ds(0, DEV - 1)], sems.at[2])
    wait_bytes(rows_out.at[pl.ds(0, 16 * (DEV - 1))], sems.at[4])


VMEM = pl.BlockSpec(memory_space=pltpu.VMEM)
ANY = pl.BlockSpec(memory_space=pl.ANY)


def fetch(owner, row, seg, table):
    return pl.pallas_call(
        fetch_kernel,
        out_shape=(
            jax.ShapeDtypeStruct((TOK, WIDTH), BF),
            jax.ShapeDtypeStruct((8, SLOTS), jnp.int32),
            jax.ShapeDtypeStruct((8, TOK), jnp.int32),
            jax.ShapeDtypeStruct((8, 128), jnp.int32),
        ),
        in_specs=[VMEM, VMEM, VMEM, ANY],
        out_specs=(VMEM, VMEM, VMEM, VMEM),
        scratch_shapes=[
            pltpu.VMEM((ROWS, WIDTH), BF),
            pltpu.VMEM((DEV, 1, 128), jnp.int32),
            pltpu.VMEM((DEV, 1, 128), jnp.int32),
            pltpu.VMEM((SLOTS, 128), jnp.int32),
            pltpu.VMEM((2 * SLOTS, WIDTH // 2), BF),
            pltpu.VMEM((2 * SLOTS, WIDTH // 2), BF),
            pltpu.VMEM((8, 128), F32),
            pltpu.VMEM((NB, 8, 128), F32),
            pltpu.SemaphoreType.DMA((6,)),
            pltpu.SemaphoreType.DMA((NB,)),
            pltpu.SemaphoreType.DMA((NB,)),
        ],
        compiler_params=pltpu.CompilerParams(
            collective_id=0, has_side_effects=True, vmem_limit_bytes=48 << 20
        ),
        name="fetch_rows",
    )(owner, row, seg, table)


HEADS = 4
DH = 64
HD = HEADS * DH
GROUP = TOK * NB
NORM_EPS = 1e-06
SPAN = 3


def dot_rows(a, b):
    return lax.dot_general(a, b, (((0,), (0,)), ((), ())), preferred_element_type=F32)


def fold(rows):
    half = rows.shape[0] // 2
    return jnp.concatenate([rows[:half], rows[half:]], axis=1)


def unfold(rows):
    return jnp.concatenate([rows[:, :DH], rows[:, DH:]], axis=0)


def normalise(values):
    centred = values - jnp.mean(values, axis=-1, keepdims=True)
    scale = lax.rsqrt(jnp.mean(centred * centred, axis=-1, keepdims=True) + NORM_EPS)
    return centred * scale, scale


def norm_grad(grad, normed, scale):
    along = jnp.mean(grad * normed, axis=-1, keepdims=True)
    return scale * (grad - jnp.mean(grad, axis=-1, keepdims=True) - normed * along)


def tile(i, size=TOK):
    return pl.ds(pl.multiple_of(i * size, size), size)


def layer_kernel(
    emb_ref, start_ref, w_in_ref, w_out_ref, cot_ref,
    out_ref, demb_ref, w_in_part, w_out_part,
    slope_v, gate_v, kv_out, q_out, kv_in, q_in, q_v, qt_v, begin_v,
    w_v, s_v, att_v, att_out, att_in, d_out, d_in, dt_v, dq_v, dq_out, dq_in,
    g_out, g_in, joined,
    kv_send, kv_recv, q_send, q_recv, a_send, a_recv, d_send, d_recv,
    g_send, g_recv, e_send, e_recv,
):
    b, g = lax.axis_index("bal"), lax.axis_index("grp")
    z, x = b // HEADS, lax.rem(b, HEADS)
    barrier = pltpu.get_barrier_semaphore()
    for k in range(1, NB):
        pl.semaphore_signal(
            barrier, inc=1, device_id=(lax.rem(b + k, NB), g), device_id_type=MESH
        )

    def remote(src, dst, send, recv, at_z, at_x):
        return pltpu.make_async_remote_copy(
            src_ref=src, dst_ref=dst, send_sem=send, recv_sem=recv,
            device_id=(at_z * HEADS + at_x, g), device_id_type=MESH,
        )

    def spread(out, into, send, recv):
        for h in range(HEADS):
            @pl.when(h != x)
            def _():
                remote(out.at[h], into.at[x], send.at[h], recv.at[x], z, h).start()

            @pl.when(h == x)
            def _():
                into[h] = out[h]

    def collect(out, into, send, recv):
        for h in range(HEADS):
            @pl.when(h != x)
            def _():
                remote(out.at[h], into.at[h], send.at[h], recv.at[h], z, h).wait_recv()

    def sent(out, into, send, recv):
        for h in range(HEADS):
            @pl.when(h != x)
            def _():
                remote(out.at[h], into.at[h], send.at[h], recv.at[h], z, h).wait_send()

    embedded = emb_ref[...].astype(F32)
    normed, _ = normalise(embedded)
    normed = normed.astype(BF)
    pre = dot(normed, w_in_ref[...])
    sig = jax.nn.sigmoid(pre)
    act = pre * sig
    gate_v[...] = act[:, :HD].astype(BF)
    for h in range(HEADS):
        value, query, key = (
            act[:, part * HD + h * DH : part * HD + (h + 1) * DH] for part in (1, 2, 3)
        )
        kv_out[h] = jnp.concatenate([key, value], axis=1).astype(BF)
        q_out[h] = fold(query * 0.5).astype(BF)
    pl.semaphore_wait(barrier, NB - 1)
    spread(q_out, q_in, q_send, q_recv)
    for dz in range(SPAN):
        for h in range(HEADS):
            @pl.when((z + dz < HEADS) & ((h != x) | (dz > 0)))
            def _():
                remote(
                    kv_out.at[h], kv_in.at[dz, x], kv_send.at[dz, h], kv_recv.at[dz, x], z + dz, h
                ).start()

            if dz == 0:
                @pl.when(h == x)
                def _():
                    kv_in[0, h] = kv_out[h]

    slope_v[...] = sig * (1.0 + pre * (1.0 - sig))
    att_v[...] = jnp.zeros_like(att_v)
    dq_v[...] = jnp.zeros_like(dq_v)
    places = z * HEADS * TOK + iota((HEADS * TOK, 128), 0)
    starts = start_ref[:1, :]
    begin = jnp.max(jnp.where(starts <= places, starts, 0).astype(F32), axis=1, keepdims=True)
    begin_v[...] = jnp.broadcast_to(begin, (HEADS * TOK, 128)).astype(jnp.int32)
    collect(q_out, q_in, q_send, q_recv)
    for h in range(HEADS):
        q = unfold(q_in[h].astype(F32))
        q_v[h * TOK : (h + 1) * TOK, :] = jnp.concatenate(
            [q, jnp.zeros((TOK, DH), F32)], axis=1
        ).astype(BF)
        qt_v[:, h * TOK : (h + 1) * TOK] = q.T.astype(BF)

    def forward_pair(dz, i, j):
        kv = kv_in[dz, j]
        scores = dot_t(q_v[tile(i), :], kv)
        half = jnp.tanh(scores)
        more = 1.0 + half
        key_pos = ((z - dz) * HEADS + j) * TOK + iota((TOK, TOK), 1)
        visible = key_pos >= begin_v[tile(i), :1]
        if dz == 0:
            visible &= key_pos <= (z * HEADS + i) * TOK + iota((TOK, TOK), 0)
        weight = jnp.where(visible, scores * more, 0.0).astype(BF)
        w_v[dz, i * HEADS + j] = weight
        s_v[dz, i * HEADS + j] = jnp.where(
            visible, more * (1.0 + scores * (1.0 - half)), 0.0
        ).astype(BF)
        att_v[tile(i), :] += dot(weight, kv)

    def arrived(dz):
        for h in range(HEADS):
            def arrival():
                remote(
                    kv_out.at[h], kv_in.at[dz, h], kv_send.at[dz, h], kv_recv.at[dz, h], z, h
                ).wait_recv()

            if dz == 0:
                pl.when(h != x)(arrival)
            else:
                arrival()

    def sweep(body, dz):
        def outer(i, carry):
            low = 0 if dz < 2 else i
            high = i + 1 if dz == 0 else HEADS

            def inner(j, carry):
                body(dz, i, j)
                return carry

            return lax.fori_loop(low, high, inner, carry)

        lax.fori_loop(0, HEADS, outer, 0)

    for dz in range(SPAN):
        @pl.when(z >= dz)
        def _():
            arrived(dz)
            sweep(forward_pair, dz)

    for h in range(HEADS):
        att = att_v[h * TOK : (h + 1) * TOK, DH:] * (2.0 / GROUP)
        att_out[h] = fold(att).astype(BF)
    spread(att_out, att_in, a_send, a_recv)
    cot = cot_ref[...]
    d_mixed = dot_t(cot, w_out_ref[...])
    gate = gate_v[...].astype(F32)
    collect(att_out, att_in, a_send, a_recv)

    attended = jnp.concatenate([unfold(att_in[h].astype(F32)) for h in range(HEADS)], axis=1)
    level, scale = normalise(attended)
    delta = norm_grad(d_mixed * gate, level, scale)
    for h in range(HEADS):
        d_out[h] = fold(delta[:, h * DH : (h + 1) * DH]).astype(BF)
    spread(d_out, d_in, d_send, d_recv)
    mixed = (level * gate).astype(BF)
    out_ref[...] = (dot(mixed, w_out_ref[...]) + emb_ref[...].astype(F32)).astype(BF)
    w_out_part[...] = dot_rows(mixed, cot).astype(w_out_part.dtype)
    joined[:, :HD] = (d_mixed * level).astype(BF)
    collect(d_out, d_in, d_send, d_recv)
    for h in range(HEADS):
        d = unfold(d_in[h].astype(F32))
        q_v[HEADS * TOK + h * TOK : HEADS * TOK + (h + 1) * TOK, :] = jnp.concatenate(
            [jnp.zeros((TOK, DH), F32), d], axis=1
        ).astype(BF)
        dt_v[:, h * TOK : (h + 1) * TOK] = d.T.astype(BF)

    def backward(dz):
        def keys(j, carry):
            kv = kv_in[dz, j]

            def queries(i, grads):
                dk, dv = grads
                product = dot_t(q_v[tile(HEADS + i), :], kv)
                d_score = (product * s_v[dz, i * HEADS + j].astype(F32)).astype(BF)
                dq_v[tile(i), :] += dot(d_score, kv)
                dk = dk + dot(qt_v[:, tile(i)], d_score)
                dv = dv + dot(dt_v[:, tile(i)], w_v[dz, i * HEADS + j])
                return dk, dv

            low = j if dz == 0 else 0
            high = j + 1 if dz == 2 else HEADS
            zeros = jnp.zeros((DH, TOK), F32)
            dk, dv = lax.fori_loop(low, high, queries, (zeros, zeros))
            grads = jnp.concatenate([dk, dv], axis=0) * (2.0 / GROUP)
            g_out[dz, j] = grads.T.astype(BF)
            if dz == 0:
                @pl.when(j != x)
                def _():
                    remote(
                        g_out.at[0, j], g_in.at[0, x], g_send.at[0, j], g_recv.at[0, x], z, j
                    ).start()

                @pl.when(j == x)
                def _():
                    g_in[0, j] = g_out[0, j]
            else:
                remote(
                    g_out.at[dz, j], g_in.at[dz, x], g_send.at[dz, j], g_recv.at[dz, x], z - dz, j
                ).start()
            return carry

        lax.fori_loop(0, HEADS, keys, 0)

    for dz in reversed(range(SPAN)):
        @pl.when(z >= dz)
        def _():
            backward(dz)

    for h in range(HEADS):
        dq_out[h] = fold(dq_v[h * TOK : (h + 1) * TOK, :DH] * (1.0 / GROUP)).astype(BF)
    spread(dq_out, dq_in, e_send, e_recv)

    embedded = emb_ref[...].astype(F32)
    spread_in, spread_scale = normalise(embedded)
    normed = spread_in.astype(BF)
    for dz in reversed(range(SPAN)):
        for h in range(HEADS):
            def arrival():
                remote(
                    g_out.at[dz, h], g_in.at[dz, h], g_send.at[dz, h], g_recv.at[dz, h], z, h
                ).wait_recv()

            if dz == 0:
                pl.when(h != x)(arrival)
            else:
                pl.when(z + dz < HEADS)(arrival)

    collect(dq_out, dq_in, e_send, e_recv)
    for h in range(HEADS):
        total = g_in[0, h].astype(F32)
        for dz in range(1, SPAN):
            total += jnp.where(z + dz < HEADS, g_in[dz, h].astype(F32), 0.0)
        joined[:, HD + h * DH : HD + (h + 1) * DH] = total[:, DH:].astype(BF)
        joined[:, 2 * HD + h * DH : 2 * HD + (h + 1) * DH] = unfold(
            dq_in[h].astype(F32)
        ).astype(BF)
        joined[:, 3 * HD + h * DH : 3 * HD + (h + 1) * DH] = total[:, :DH].astype(BF)
    d_pre = (joined[...].astype(F32) * slope_v[...]).astype(BF)
    w_in_part[...] = dot_rows(normed, d_pre).astype(w_in_part.dtype)
    d_normed = dot_t(d_pre, w_in_ref[...])
    demb_ref[...] = (
        norm_grad(d_normed, spread_in, spread_scale) + cot_ref[...].astype(F32)
    ).astype(BF)

    sent(q_out, q_in, q_send, q_recv)
    sent(att_out, att_in, a_send, a_recv)
    sent(d_out, d_in, d_send, d_recv)
    sent(dq_out, dq_in, e_send, e_recv)
    for dz in range(SPAN):
        for h in range(HEADS):
            @pl.when((z + dz < HEADS) & ((h != x) | (dz > 0)))
            def _():
                remote(
                    kv_out.at[h], kv_in.at[dz, h], kv_send.at[dz, h], kv_recv.at[dz, h], z, h
                ).wait_send()

            @pl.when((z >= dz) & ((h != x) | (dz > 0)))
            def _():
                remote(
                    g_out.at[dz, h], g_in.at[dz, h], g_send.at[dz, h], g_recv.at[dz, h], z, h
                ).wait_send()


def layer(embedded, start, w_in, w_out, cot, part_type):
    dma = pltpu.SemaphoreType.DMA
    return pl.pallas_call(
        layer_kernel,
        out_shape=(
            jax.ShapeDtypeStruct((TOK, WIDTH), BF),
            jax.ShapeDtypeStruct((TOK, WIDTH), BF),
            jax.ShapeDtypeStruct((WIDTH, 4 * HD), part_type),
            jax.ShapeDtypeStruct((HD, WIDTH), part_type),
        ),
        in_specs=[VMEM] * 5,
        out_specs=(VMEM,) * 4,
        scratch_shapes=[
            pltpu.VMEM((TOK, 4 * HD), F32),
            pltpu.VMEM((TOK, HD), BF),
            pltpu.VMEM((HEADS, TOK, 2 * DH), BF),
            pltpu.VMEM((HEADS, TOK // 2, 2 * DH), BF),
            pltpu.VMEM((SPAN, HEADS, TOK, 2 * DH), BF),
            pltpu.VMEM((HEADS, TOK // 2, 2 * DH), BF),
            pltpu.VMEM((2 * HEADS * TOK, 2 * DH), BF),
            pltpu.VMEM((DH, HEADS * TOK), BF),
            pltpu.VMEM((HEADS * TOK, 128), jnp.int32),
            pltpu.VMEM((SPAN, HEADS * HEADS, TOK, TOK), BF),
            pltpu.VMEM((SPAN, HEADS * HEADS, TOK, TOK), BF),
            pltpu.VMEM((HEADS * TOK, 2 * DH), F32),
            pltpu.VMEM((HEADS, TOK // 2, 2 * DH), BF),
            pltpu.VMEM((HEADS, TOK // 2, 2 * DH), BF),
            pltpu.VMEM((HEADS, TOK // 2, 2 * DH), BF),
            pltpu.VMEM((HEADS, TOK // 2, 2 * DH), BF),
            pltpu.VMEM((DH, HEADS * TOK), BF),
            pltpu.VMEM((HEADS * TOK, 2 * DH), F32),
            pltpu.VMEM((HEADS, TOK // 2, 2 * DH), BF),
            pltpu.VMEM((HEADS, TOK // 2, 2 * DH), BF),
            pltpu.VMEM((SPAN, HEADS, TOK, 2 * DH), BF),
            pltpu.VMEM((SPAN, HEADS, TOK, 2 * DH), BF),
            pltpu.VMEM((TOK, 4 * HD), BF),
            dma((SPAN, HEADS)),
            dma((SPAN, HEADS)),
        ]
        + [dma((HEADS,))] * 6
        + [dma((SPAN, HEADS))] * 2
        + [dma((HEADS,))] * 2,
        compiler_params=pltpu.CompilerParams(
            collective_id=2, has_side_effects=True, vmem_limit_bytes=56 << 20
        ),
        name="layer",
    )(embedded, start, w_in, w_out, cot)


def return_kernel(slot_ref, grad_ref, landed_ref, out_v, in_v, sems):
    b, g = lax.axis_index("bal"), lax.axis_index("grp")
    me = b * NG + g
    barrier = greet_all(me)
    part = SLOTS // 4
    peers = DEV // 4
    pl.semaphore_wait(barrier, DEV - 1)

    def serve(i, carry):
        c = lax.rem(me // peers + i, 4)
        chosen = hot(slot_ref[:1, :] == iota((part, TOK), 0) + c * part)
        found = paired_halves(dot(chosen, grad_ref[...]))
        out_v[pl.ds(pl.multiple_of(c * 2 * part, 2 * part), 2 * part), :] = found

        def give(k, inner):
            p = c * peers + lax.rem(me + k, peers)

            @pl.when(p != me)
            def _():
                pltpu.make_async_remote_copy(
                    src_ref=out_v.at[pl.ds(pl.multiple_of(p * 16, 16), 16)],
                    dst_ref=in_v.at[pl.ds(pl.multiple_of(me * 16, 16), 16)],
                    send_sem=sems.at[0], recv_sem=sems.at[1],
                    device_id=device(p), device_id_type=MESH,
                ).start()

            return inner

        return lax.fori_loop(0, peers, give, carry)

    lax.fori_loop(0, 4, serve, 0)
    home = pl.ds(pl.multiple_of(me * 16, 16), 16)
    own = pltpu.make_async_copy(out_v.at[home], in_v.at[home], sems.at[2])
    own.start()
    own.wait()
    wait_bytes(in_v.at[pl.ds(0, 16 * (DEV - 1))], sems.at[1])
    halves = in_v[...].astype(F32).reshape(DEV, 2 * CAP, WIDTH // 2)
    whole = jnp.concatenate([halves[:, :CAP], halves[:, CAP:]], axis=2)
    landed_ref[...] = whole.reshape(SLOTS, WIDTH).astype(BF)
    wait_bytes(out_v.at[pl.ds(0, 16 * (DEV - 1))], sems.at[0])


def give_back(slot, grad):
    return pl.pallas_call(
        return_kernel,
        out_shape=jax.ShapeDtypeStruct((SLOTS, WIDTH), BF),
        in_specs=[VMEM, VMEM],
        out_specs=VMEM,
        scratch_shapes=[
            pltpu.VMEM((2 * SLOTS, WIDTH // 2), BF),
            pltpu.VMEM((2 * SLOTS, WIDTH // 2), BF),
            pltpu.SemaphoreType.DMA((3,)),
        ],
        compiler_params=pltpu.CompilerParams(
            collective_id=1, has_side_effects=True, vmem_limit_bytes=48 << 20
        ),
        name="return_grads",
    )(slot, grad)


def scatter_kernel(want_ref, landed_ref, out_ref):
    part = out_ref.shape[0]
    rows = iota((part, SLOTS), 0) + pl.program_id(0) * part
    out_ref[...] = dot(hot(want_ref[:1, :] == rows), landed_ref[...])


def scatter_add(want, landed):
    part = 256
    return pl.pallas_call(
        scatter_kernel,
        grid=(ROWS // part,),
        out_shape=jax.ShapeDtypeStruct((ROWS, WIDTH), F32),
        in_specs=[
            pl.BlockSpec((8, SLOTS), lambda i: (0, 0)),
            pl.BlockSpec((SLOTS, WIDTH), lambda i: (0, 0)),
        ],
        out_specs=pl.BlockSpec((part, WIDTH), lambda i: (i, 0)),
        compiler_params=pltpu.CompilerParams(vmem_limit_bytes=32 << 20),
        name="scatter_rows",
    )(want, landed)


def per_device(table, item_owner, item_row, segment, w_in, w_out, cotangent):
    embedded, want, slot, start = fetch(item_owner[0], item_row, segment, table)
    layer_out, d_embedded, w_in_part, w_out_part = layer(
        embedded, start, w_in, w_out, cotangent[0], F32
    )
    landed = give_back(slot, d_embedded)
    table_grad = scatter_add(want, landed)
    w_in_grad, w_out_grad = lax.psum((w_in_part, w_out_part), ("bal", "grp"))
    return (layer_out[None], table_grad, w_in_grad, w_out_grad)


def solution(mesh):
    placed = (
        P(("bal", "grp"), None),
        P("grp", "bal", None),
        P("grp", "bal"),
        P("grp", "bal"),
        P(),
        P(),
        P("grp", "bal", None),
    )
    return jax.shard_map(
        per_device,
        mesh=mesh,
        in_specs=placed,
        out_specs=(P("grp", "bal", None), P(("bal", "grp"), None), P(), P()),
        check_vma=False,
    )
```

```python
import functools
import types

import jax
import jax.numpy as jnp
from jax import lax
from jax.experimental import pallas as pl
from jax.experimental.pallas import tpu as pltpu
from jax.sharding import PartitionSpec as P

MESH = pl.DeviceIdType.MESH
BF = jnp.bfloat16
F32 = jnp.float32
TOK = 256
WIDTH = 512
CAP = 8
ROWS = 2048
NB = 16
NG = 8
DEV = NB * NG
SLOTS = DEV * CAP


def iota(shape, dim):
    return lax.broadcasted_iota(jnp.int32, shape, dim)


def hot(mask):
    return jnp.where(mask, 1.0, 0.0).astype(BF)


def dot(a, b):
    return jnp.dot(a, b, preferred_element_type=F32)


def dot_t(a, b):
    return lax.dot_general(a, b, (((1,), (1,)), ((), ())), preferred_element_type=F32)


def column_of(line):
    size = line.shape[1]
    eye = iota((size, size), 0) == iota((size, size), 1)
    return jnp.sum(jnp.where(eye, line, 0.0), axis=1, keepdims=True)


def line_of(column):
    size = column.shape[0]
    eye = iota((size, size), 0) == iota((size, size), 1)
    return jnp.sum(jnp.where(eye, column, 0.0), axis=0, keepdims=True)


def device(p):
    return (p // NG, lax.rem(p, NG))


def greet_all(me):
    barrier = pltpu.get_barrier_semaphore()

    def greet(k, carry):
        pl.semaphore_signal(
            barrier, inc=1, device_id=device(lax.rem(me + k, DEV)), device_id_type=MESH
        )
        return carry

    lax.fori_loop(1, DEV, greet, 0)
    return barrier


def paired_halves(rows):
    count = rows.shape[0] // CAP
    split = rows.reshape(count, CAP, WIDTH)
    joined = jnp.concatenate([split[:, :, : WIDTH // 2], split[:, :, WIDTH // 2 :]], axis=1)
    return joined.reshape(count * 2 * CAP, WIDTH // 2).astype(BF)


def wait_bytes(view, sem):
    pltpu.make_async_copy(view, view, sem).wait()


HEADS = 4
DH = 64
HD = HEADS * DH
GROUP = TOK * NB
NORM_EPS = 1e-06
SPAN = 3
ATT = F32


def dot_rows(a, b):
    return lax.dot_general(a, b, (((0,), (0,)), ((), ())), preferred_element_type=F32)


def fold(rows):
    half = rows.shape[0] // 2
    return jnp.concatenate([rows[:half], rows[half:]], axis=1)


def unfold(rows):
    return jnp.concatenate([rows[:, :DH], rows[:, DH:]], axis=0)


def normalise(values):
    centred = values - jnp.mean(values, axis=-1, keepdims=True)
    scale = lax.rsqrt(jnp.mean(centred * centred, axis=-1, keepdims=True) + NORM_EPS)
    return centred * scale, scale


def norm_grad(grad, normed, scale):
    along = jnp.mean(grad * normed, axis=-1, keepdims=True)
    return scale * (grad - jnp.mean(grad, axis=-1, keepdims=True) - normed * along)


def tile(i, size=TOK):
    return pl.ds(pl.multiple_of(i * size, size), size)


def fetch_rows(r, me, b, g, barrier):
    owner = r.owner[...]
    owner_f = owner.astype(F32)
    lanes = iota((TOK, 128), 1)
    named = jnp.where(owner == lanes, 1.0, 0.0)
    before = hot(iota((TOK, TOK), 0) > iota((TOK, TOK), 1))
    rank = jnp.sum(dot(before, named.astype(BF)) * named, axis=1, keepdims=True)
    slot = owner_f * CAP + rank
    r.slot[...] = jnp.broadcast_to(line_of(slot), (8, TOK)).astype(jnp.int32)
    ask = column_of(r.row[...].astype(F32)) + 1.0
    high = jnp.floor(ask * (1.0 / 64.0))
    low = ask - 64.0 * high
    mine = rank.astype(jnp.int32) == lanes // 16
    named_t = hot(line_of(owner_f).astype(jnp.int32) == iota((DEV, TOK), 0))
    r.asked[...] = (
        64.0 * dot(named_t, jnp.where(mine, high, 0.0).astype(BF))
        + dot(named_t, jnp.where(mine, low, 0.0).astype(BF))
    ).astype(jnp.int32).reshape(DEV, 1, 128)
    seg = column_of(r.seg[...].astype(F32)).astype(jnp.int32)
    below = jnp.sum(jnp.where(seg < lanes, 1.0, 0.0), axis=0, keepdims=True)
    r.count_out[...] = jnp.broadcast_to(below, (8, 128))
    r.count_in[b] = jnp.broadcast_to(below, (8, 128))
    own = pltpu.make_async_copy(r.asked.at[me], r.asks.at[me], r.sems.at[1])
    own.start()
    own.wait()
    pl.semaphore_wait(barrier, DEV - 1)

    def ask_for(k, carry):
        p = lax.rem(me + k, DEV)
        pltpu.make_async_remote_copy(
            src_ref=r.asked.at[p], dst_ref=r.asks.at[me], send_sem=r.sems.at[2],
            recv_sem=r.sems.at[3], device_id=device(p), device_id_type=MESH,
        ).start()
        return carry

    lax.fori_loop(1, DEV, ask_for, 0)
    tallies = []
    for k in range(1, NB):
        tally = pltpu.make_async_remote_copy(
            src_ref=r.count_out, dst_ref=r.count_in.at[b], send_sem=r.count_send.at[k],
            recv_sem=r.count_recv.at[k], device_id=(lax.rem(b + k, NB), g), device_id_type=MESH,
        )
        tally.start()
        tallies.append(tally)
    for k, (source, into) in enumerate(r.loads):
        pltpu.make_async_copy(source, into, r.load_sems.at[k]).wait()
    wait_bytes(r.asks.at[pl.ds(0, DEV - 1)], r.sems.at[3])
    got = r.asks[...].reshape(DEV, 128).astype(F32)
    got_high = jnp.floor(got * (1.0 / 64.0))
    got_low = got - 64.0 * got_high
    spread = hot(iota((SLOTS, DEV), 0) // CAP == iota((SLOTS, DEV), 1))
    every = 64.0 * dot(spread, got_high.astype(BF)) + dot(spread, got_low.astype(BF))
    pick = lax.rem(iota((SLOTS, 128), 0), CAP) * 16 == iota((SLOTS, 128), 1)
    want = jnp.sum(jnp.where(pick, every, 0.0), axis=1, keepdims=True) - 1.0
    want = jnp.broadcast_to(want, (SLOTS, 128))
    r.want_v[...] = want.astype(jnp.int32)

    def rows_of(first, count):
        rows = r.want_v[pl.ds(first, count), :]
        return dot(hot(rows[:, :1] == iota((count, ROWS), 1)), r.table_v[...])

    exchange_rows(me, rows_of, r.rows_out, r.rows_in, r.sems.at[4], r.sems.at[5], r.sems.at[1])
    r.want[...] = want.T[:8].astype(jnp.int32)
    for tally in tallies:
        tally.wait()
    total = jnp.sum(r.count_in[...], axis=0)
    r.start[...] = total.astype(jnp.int32)
    slot = slot.astype(jnp.int32)
    place = (slot // CAP) * 16 + lax.rem(slot, CAP)
    spots = iota((TOK, 2 * SLOTS), 1)
    left, right = hot(place == spots), hot(place + CAP == spots)
    wait_bytes(r.rows_in.at[pl.ds(0, 16 * (DEV - 1))], r.sems.at[5])
    r.emb[:, : WIDTH // 2] = dot(left, r.rows_in[...]).astype(BF)
    r.emb[:, WIDTH // 2 :] = dot(right, r.rows_in[...]).astype(BF)


def exchange_rows(me, rows_of, out, into, send, recv, local):
    part = SLOTS // 4
    peers = DEV // 4

    def serve(i, carry):
        c = lax.rem(me // peers + i, 4)
        found = paired_halves(rows_of(pl.multiple_of(c * part, part), part))
        out[pl.ds(pl.multiple_of(c * 2 * part, 2 * part), 2 * part), :] = found

        def give(k, inner):
            p = c * peers + lax.rem(me + k, peers)

            @pl.when(p != me)
            def _():
                pltpu.make_async_remote_copy(
                    src_ref=out.at[pl.ds(pl.multiple_of(p * 16, 16), 16)],
                    dst_ref=into.at[pl.ds(pl.multiple_of(me * 16, 16), 16)],
                    send_sem=send, recv_sem=recv, device_id=device(p), device_id_type=MESH,
                ).start()

            return inner

        return lax.fori_loop(0, peers, give, carry)

    lax.fori_loop(0, 4, serve, 0)
    home = pl.ds(pl.multiple_of(me * 16, 16), 16)
    own = pltpu.make_async_copy(out.at[home], into.at[home], local)
    own.start()
    own.wait()


class Reduction:
    def __init__(self, r, which, width, part, core_in, held, first_in, second_in, last_in, full):
        self.r, self.which, self.width = r, which, width
        self.part, self.core_in, self.held = part, core_in, held
        self.first_in, self.second_in, self.last_in, self.full = (
            first_in, second_in, last_in, full,
        )
        b, g = lax.axis_index("bal"), lax.axis_index("grp")
        self.core = lax.rem(g, 2)
        y, x, z = g // 2, lax.rem(b, HEADS), b // HEADS
        self.twin = (b, g + 1 - 2 * self.core)
        self.axes = (
            (y, lambda p: (b, p * 2 + self.core)),
            (x, lambda p: (z * HEADS + p, g)),
            (z, lambda p: (p * HEADS + x, g)),
        )

    def columns(self, half):
        return pl.ds(half * self.width // 2, self.width // 2)

    def order(self, half):
        return (self.axes[half], self.axes[1 - half], self.axes[2])

    def copies(self, phase, half, axis, src, dst):
        here, device_of = axis
        out = []
        for k in range(1, HEADS):
            p = lax.rem(here + k, HEADS)
            out.append(
                pltpu.make_async_remote_copy(
                    src_ref=src(p), dst_ref=dst(here),
                    send_sem=self.r.red_send.at[self.which, phase, half, p],
                    recv_sem=self.r.red_recv.at[self.which, phase, half, here],
                    device_id=device_of(p), device_id_type=MESH,
                )
            )
        return out

    def views(self, phase, half):
        first, second, last = self.order(half)
        columns = self.columns(half)
        base = self.core * TOK
        if phase == 0:
            return (
                first,
                lambda p: self.held.at[pl.ds(pl.multiple_of(p * 64, 64), 64), columns],
                lambda p: self.first_in.at[half, p],
            )
        if phase == 1:
            return (
                second,
                lambda p: self.first_in.at[half, first[0], pl.ds(pl.multiple_of(p * 16, 16), 16)],
                lambda p: self.second_in.at[half, p],
            )
        if phase == 2:
            return (
                last,
                lambda p: self.last_in.at[half, last[0]],
                lambda p: self.last_in.at[half, p],
            )
        if phase == 3:
            def piece(p):
                row = pl.multiple_of(base + first[0] * 64 + p * 16, 16)
                return self.full.at[pl.ds(row, 16), columns]

            return second, lambda p: piece(second[0]), piece

        def block(p):
            return self.full.at[pl.ds(pl.multiple_of(base + p * 64, 64), 64), columns]

        return first, lambda p: block(first[0]), block

    def start(self, phase):
        for half in (0, 1):
            for copy in self.copies(phase, half, *self.views(phase, half)):
                copy.start()

    def take(self, phase, half):
        axis, src, dst = self.views(phase, half)
        here, device_of = axis
        for k in range(1, HEADS):
            p = lax.rem(here + k, HEADS)
            pltpu.make_async_remote_copy(
                src_ref=src(p), dst_ref=dst(p),
                send_sem=self.r.red_send.at[self.which, phase, half, p],
                recv_sem=self.r.red_recv.at[self.which, phase, half, p],
                device_id=device_of(p), device_id_type=MESH,
            ).wait_recv()

    def core_copy(self, back):
        rows = pl.ds(pl.multiple_of((1 - self.core) * TOK, TOK), TOK)
        if back:
            rows = pl.ds(pl.multiple_of(self.core * TOK, TOK), TOK)
        return pltpu.make_async_remote_copy(
            src_ref=(self.full if back else self.part).at[rows],
            dst_ref=self.full.at[rows] if back else self.core_in,
            send_sem=self.r.twin_send.at[self.which, back],
            recv_sem=self.r.twin_recv.at[self.which, back],
            device_id=self.twin, device_id_type=MESH,
        )

    def step(self, number):
        if number == 0:
            self.core_copy(0).start()
        elif number == 1:
            self.core_copy(0).wait_recv()
            rows = pl.ds(pl.multiple_of(self.core * TOK, TOK), TOK)
            self.held[...] = (
                self.part[rows, :].astype(F32) + self.core_in[...].astype(F32)
            ).astype(BF)
            self.start(0)
        elif number == 2:
            for half in (0, 1):
                here = self.order(half)[0][0]
                own = self.held[pl.ds(pl.multiple_of(here * 64, 64), 64), self.columns(half)]
                self.first_in[half, here] = own
                self.take(0, half)
                total = self.first_in[half, 0].astype(F32)
                for p in range(1, HEADS):
                    total += self.first_in[half, p].astype(F32)
                self.first_in[half, here] = total.astype(BF)
            self.start(1)
        elif number == 3:
            for half in (0, 1):
                first, second, last = self.order(half)
                rows = pl.ds(pl.multiple_of(second[0] * 16, 16), 16)
                self.second_in[half, second[0]] = self.first_in[half, first[0], rows]
                self.take(1, half)
                total = self.second_in[half, 0].astype(F32)
                for p in range(1, HEADS):
                    total += self.second_in[half, p].astype(F32)
                self.last_in[half, last[0]] = total.astype(BF)
            self.start(2)
        elif number == 4:
            for half in (0, 1):
                first, second, _ = self.order(half)
                self.take(2, half)
                total = self.last_in[half, 0].astype(F32)
                for p in range(1, HEADS):
                    total += self.last_in[half, p].astype(F32)
                row = pl.multiple_of(self.core * TOK + first[0] * 64 + second[0] * 16, 16)
                self.full[pl.ds(row, 16), self.columns(half)] = total.astype(BF)
            self.start(3)
        elif number == 5:
            for half in (0, 1):
                self.take(3, half)
            self.start(4)
        elif number == 6:
            for half in (0, 1):
                self.take(4, half)
            self.core_copy(1).start()
        else:
            rows = pl.ds(pl.multiple_of((1 - self.core) * TOK, TOK), TOK)
            pltpu.make_async_remote_copy(
                src_ref=self.full.at[rows], dst_ref=self.full.at[rows],
                send_sem=self.r.twin_send.at[self.which, 1],
                recv_sem=self.r.twin_recv.at[self.which, 1],
                device_id=self.twin, device_id_type=MESH,
            ).wait_recv()

    def finish(self):
        for back in (0, 1):
            self.core_copy(back).wait_send()
        for phase in range(5):
            for half in (0, 1):
                for copy in self.copies(phase, half, *self.views(phase, half)):
                    copy.wait_send()


def whole_kernel(names, *refs):
    r = types.SimpleNamespace(**dict(zip(names, refs)))
    b, g = lax.axis_index("bal"), lax.axis_index("grp")
    me = b * NG + g
    barrier = greet_all(me)
    r.loads = (
        (r.table_hbm, r.table_v), (r.w_in_hbm, r.w_in), (r.w_out_hbm, r.w_out), (r.cot_hbm, r.cot),
    )
    for k, (source, into) in enumerate(r.loads):
        pltpu.make_async_copy(source, into, r.load_sems.at[k]).start()
    fetch_rows(r, me, b, g, barrier)
    early = Reduction(
        r, 0, WIDTH, r.early_part, r.early_core, r.early_held, r.early_first, r.early_second,
        r.early_last, r.early_full,
    )
    late = Reduction(
        r, 1, 3 * HD, r.late_part, r.late_core, r.late_held, r.late_first, r.late_second,
        r.late_last, r.late_full,
    )
    z, x = b // HEADS, lax.rem(b, HEADS)
    def remote(src, dst, send, recv, at_z, at_x):
        return pltpu.make_async_remote_copy(
            src_ref=src, dst_ref=dst, send_sem=send, recv_sem=recv,
            device_id=(at_z * HEADS + at_x, g), device_id_type=MESH,
        )

    def spread(out, into, send, recv):
        for h in range(HEADS):
            @pl.when(h != x)
            def _():
                remote(out.at[h], into.at[x], send.at[h], recv.at[x], z, h).start()

            @pl.when(h == x)
            def _():
                into[h] = out[h]

    def collect(out, into, send, recv):
        for h in range(HEADS):
            @pl.when(h != x)
            def _():
                remote(out.at[h], into.at[h], send.at[h], recv.at[h], z, h).wait_recv()

    def sent(out, into, send, recv):
        for h in range(HEADS):
            @pl.when(h != x)
            def _():
                remote(out.at[h], into.at[h], send.at[h], recv.at[h], z, h).wait_send()

    embedded = r.emb[...].astype(F32)
    normed, _ = normalise(embedded)
    normed = normed.astype(BF)
    pre = dot(normed, r.w_in[...])
    sig = jax.nn.sigmoid(pre)
    act = pre * sig
    r.gate_v[...] = act[:, :HD].astype(BF)
    for h in range(HEADS):
        value, query, key = (
            act[:, part * HD + h * DH : part * HD + (h + 1) * DH] for part in (1, 2, 3)
        )
        r.kv_out[h] = jnp.concatenate([key, value], axis=1).astype(BF)
        r.q_out[h] = fold(query * 0.5).astype(BF)
    spread(r.q_out, r.q_in, r.q_send, r.q_recv)
    for dz in range(SPAN):
        for h in range(HEADS):
            @pl.when((z + dz < HEADS) & ((h != x) | (dz > 0)))
            def _():
                remote(
                    r.kv_out.at[h], r.kv_in.at[dz, x], r.kv_send.at[dz, h], r.kv_recv.at[dz, x], z + dz, h
                ).start()

            if dz == 0:
                @pl.when(h == x)
                def _():
                    r.kv_in[0, h] = r.kv_out[h]

    r.slope_v[...] = sig * (1.0 + pre * (1.0 - sig))
    r.att_v[...] = jnp.zeros_like(r.att_v)
    r.dq_v[...] = jnp.zeros_like(r.dq_v)
    places = z * HEADS * TOK + iota((HEADS * TOK, 128), 0)
    starts = r.start[:1, :]
    begin = jnp.max(jnp.where(starts <= places, starts, 0).astype(F32), axis=1, keepdims=True)
    r.begin_v[...] = jnp.broadcast_to(begin, (HEADS * TOK, 128)).astype(jnp.int32)
    collect(r.q_out, r.q_in, r.q_send, r.q_recv)
    for h in range(HEADS):
        q = unfold(r.q_in[h].astype(F32))
        r.q_v[h * TOK : (h + 1) * TOK, :] = jnp.concatenate(
            [q, jnp.zeros((TOK, DH), F32)], axis=1
        ).astype(BF)
        r.qt_v[:, h * TOK : (h + 1) * TOK] = q.T.astype(BF)

    def forward_pair(dz, i, j):
        kv = r.kv_in[dz, j]
        scores = dot_t(r.q_v[tile(i), :], kv)
        half = jnp.tanh(scores)
        more = 1.0 + half
        key_pos = ((z - dz) * HEADS + j) * TOK + iota((TOK, TOK), 1)
        visible = key_pos >= r.begin_v[tile(i), :1]
        if dz == 0:
            visible &= key_pos <= (z * HEADS + i) * TOK + iota((TOK, TOK), 0)
        weight = jnp.where(visible, scores * more, 0.0).astype(BF)
        r.w_v[dz, i * HEADS + j] = weight
        r.s_v[dz, i * HEADS + j] = jnp.where(
            visible, more * (1.0 + scores * (1.0 - half)), 0.0
        ).astype(BF)
        r.att_v[tile(i), :] += dot(weight, kv)

    def arrived(dz):
        for h in range(HEADS):
            def arrival():
                remote(
                    r.kv_out.at[h], r.kv_in.at[dz, h], r.kv_send.at[dz, h], r.kv_recv.at[dz, h], z, h
                ).wait_recv()

            if dz == 0:
                pl.when(h != x)(arrival)
            else:
                arrival()

    def sweep(body, dz):
        def outer(i, carry):
            low = 0 if dz < 2 else i
            high = i + 1 if dz == 0 else HEADS

            def inner(j, carry):
                body(dz, i, j)
                return carry

            return lax.fori_loop(low, high, inner, carry)

        lax.fori_loop(0, HEADS, outer, 0)

    for dz in range(SPAN):
        @pl.when(z >= dz)
        def _():
            arrived(dz)
            sweep(forward_pair, dz)

    for h in range(HEADS):
        att = r.att_v[h * TOK : (h + 1) * TOK, DH:] * (2.0 / GROUP)
        r.att_out[h] = fold(att).astype(ATT)
    spread(r.att_out, r.att_in, r.a_send, r.a_recv)
    cot = r.cot[...]
    d_mixed = dot_t(cot, r.w_out[...])
    gate = r.gate_v[...].astype(F32)
    collect(r.att_out, r.att_in, r.a_send, r.a_recv)

    attended = jnp.concatenate([unfold(r.att_in[h].astype(F32)) for h in range(HEADS)], axis=1)
    level, scale = normalise(attended)
    delta = norm_grad(d_mixed * gate, level, scale)
    for h in range(HEADS):
        r.d_out[h] = fold(delta[:, h * DH : (h + 1) * DH]).astype(BF)
    spread(r.d_out, r.d_in, r.d_send, r.d_recv)
    mixed = (level * gate).astype(BF)
    r.layer_out[...] = (dot(mixed, r.w_out[...]) + r.emb[...].astype(F32)).astype(BF)
    d_gate = (d_mixed * level).astype(BF).astype(F32)
    r.joined[:, :HD] = (d_gate * r.slope_v[:, :HD]).astype(BF)
    embedded = r.emb[...].astype(F32)
    normed = normalise(embedded)[0].astype(BF)
    r.early_part[:, :HD] = dot_rows(normed, r.joined[:, :HD]).astype(BF)
    out_grad = dot_rows(mixed, cot)
    r.early_part[:HD, HD:] = out_grad[:, : WIDTH // 2].astype(BF)
    r.early_part[HD:, HD:] = out_grad[:, WIDTH // 2 :].astype(BF)
    early.step(0)
    collect(r.d_out, r.d_in, r.d_send, r.d_recv)
    for h in range(HEADS):
        d = unfold(r.d_in[h].astype(F32))
        r.q_v[HEADS * TOK + h * TOK : HEADS * TOK + (h + 1) * TOK, :] = jnp.concatenate(
            [jnp.zeros((TOK, DH), F32), d], axis=1
        ).astype(BF)
        r.dt_v[:, h * TOK : (h + 1) * TOK] = d.T.astype(BF)

    def backward(dz):
        def keys(j, carry):
            kv = r.kv_in[dz, j]

            def queries(i, grads):
                dk, dv = grads
                product = dot_t(r.q_v[tile(HEADS + i), :], kv)
                d_score = (product * r.s_v[dz, i * HEADS + j].astype(F32)).astype(BF)
                r.dq_v[tile(i), :] += dot(d_score, kv)
                dk = dk + dot(r.qt_v[:, tile(i)], d_score)
                dv = dv + dot(r.dt_v[:, tile(i)], r.w_v[dz, i * HEADS + j])
                return dk, dv

            low = j if dz == 0 else 0
            high = j + 1 if dz == 2 else HEADS
            zeros = jnp.zeros((DH, TOK), F32)
            dk, dv = lax.fori_loop(low, high, queries, (zeros, zeros))
            grads = jnp.concatenate([dk, dv], axis=0) * (2.0 / GROUP)
            r.g_out[dz, j] = grads.T.astype(BF)
            if dz == 0:
                @pl.when(j != x)
                def _():
                    remote(
                        r.g_out.at[0, j], r.g_in.at[0, x], r.g_send.at[0, j], r.g_recv.at[0, x], z, j
                    ).start()

                @pl.when(j == x)
                def _():
                    r.g_in[0, j] = r.g_out[0, j]
            else:
                remote(
                    r.g_out.at[dz, j], r.g_in.at[dz, x], r.g_send.at[dz, j], r.g_recv.at[dz, x], z - dz, j
                ).start()
            return carry

        lax.fori_loop(0, HEADS, keys, 0)

    for dz in reversed(range(SPAN)):
        @pl.when(z >= dz)
        def _():
            backward(dz)

        early.step(SPAN - dz)

    for h in range(HEADS):
        r.dq_out[h] = fold(r.dq_v[h * TOK : (h + 1) * TOK, :DH] * (1.0 / GROUP)).astype(BF)
    spread(r.dq_out, r.dq_in, r.e_send, r.e_recv)

    spread_in, spread_scale = normalise(embedded)
    normed = spread_in.astype(BF)
    for dz in reversed(range(SPAN)):
        for h in range(HEADS):
            def arrival():
                remote(
                    r.g_out.at[dz, h], r.g_in.at[dz, h], r.g_send.at[dz, h], r.g_recv.at[dz, h], z, h
                ).wait_recv()

            if dz == 0:
                pl.when(h != x)(arrival)
            else:
                pl.when(z + dz < HEADS)(arrival)

    collect(r.dq_out, r.dq_in, r.e_send, r.e_recv)
    for h in range(HEADS):
        total = r.g_in[0, h].astype(F32)
        for dz in range(1, SPAN):
            total += jnp.where(z + dz < HEADS, r.g_in[dz, h].astype(F32), 0.0)
        r.joined[:, HD + h * DH : HD + (h + 1) * DH] = total[:, DH:].astype(BF)
        r.joined[:, 2 * HD + h * DH : 2 * HD + (h + 1) * DH] = unfold(
            r.dq_in[h].astype(F32)
        ).astype(BF)
        r.joined[:, 3 * HD + h * DH : 3 * HD + (h + 1) * DH] = total[:, :DH].astype(BF)
    r.joined[:, HD:] = (r.joined[:, HD:].astype(F32) * r.slope_v[:, HD:]).astype(BF)
    r.late_part[...] = dot_rows(normed, r.joined[:, HD:]).astype(BF)
    late.step(0)
    early.step(4)
    d_normed = dot_t(r.joined[...], r.w_in[...])
    r.demb[...] = (
        norm_grad(d_normed, spread_in, spread_scale) + r.cot[...].astype(F32)
    ).astype(BF)

    def grads_of(first, count):
        return dot(hot(r.slot[:1, :] == iota((count, TOK), 0) + first), r.demb[...])

    exchange_rows(me, grads_of, r.grads_out, r.grads_in, r.sems.at[6], r.sems.at[7], r.sems.at[1])
    late.step(1)
    early.step(5)
    late.step(2)
    early.step(6)
    late.step(3)
    early.step(7)
    r.early[...] = r.early_full[...]
    for number in range(4, 8):
        late.step(number)
    r.late[...] = r.late_full[...]
    wait_bytes(r.grads_in.at[pl.ds(0, 16 * (DEV - 1))], r.sems.at[7])
    halves = r.grads_in[...].astype(F32).reshape(DEV, 2 * CAP, WIDTH // 2)
    whole = jnp.concatenate([halves[:, :CAP], halves[:, CAP:]], axis=2)
    r.landed[...] = whole.reshape(SLOTS, WIDTH).astype(BF)

    sent(r.q_out, r.q_in, r.q_send, r.q_recv)
    sent(r.att_out, r.att_in, r.a_send, r.a_recv)
    sent(r.d_out, r.d_in, r.d_send, r.d_recv)
    sent(r.dq_out, r.dq_in, r.e_send, r.e_recv)
    for dz in range(SPAN):
        for h in range(HEADS):
            @pl.when((z + dz < HEADS) & ((h != x) | (dz > 0)))
            def _():
                remote(
                    r.kv_out.at[h], r.kv_in.at[dz, h], r.kv_send.at[dz, h], r.kv_recv.at[dz, h], z, h
                ).wait_send()

            @pl.when((z >= dz) & ((h != x) | (dz > 0)))
            def _():
                remote(
                    r.g_out.at[dz, h], r.g_in.at[dz, h], r.g_send.at[dz, h], r.g_recv.at[dz, h], z, h
                ).wait_send()
    early.finish()
    late.finish()
    wait_bytes(r.asked.at[pl.ds(0, DEV - 1)], r.sems.at[2])
    wait_bytes(r.rows_out.at[pl.ds(0, 16 * (DEV - 1))], r.sems.at[4])
    wait_bytes(r.grads_out.at[pl.ds(0, 16 * (DEV - 1))], r.sems.at[6])


VMEM = pl.BlockSpec(memory_space=pltpu.VMEM)
ANY = pl.BlockSpec(memory_space=pl.ANY)


def whole(owner, row, seg, table, w_in, w_out, cot):
    dma = pltpu.SemaphoreType.DMA
    I32 = jnp.int32
    outs = dict(
        layer_out=((TOK, WIDTH), BF),
        want=((8, SLOTS), I32),
        landed=((SLOTS, WIDTH), BF),
        early=((WIDTH, WIDTH), BF),
        late=((WIDTH, 3 * HD), BF),
    )
    scratch = dict(
        table_v=((ROWS, WIDTH), BF),
        w_in=((WIDTH, 4 * HD), BF),
        w_out=((HD, WIDTH), BF),
        cot=((TOK, WIDTH), BF),
        emb=((TOK, WIDTH), BF),
        demb=((TOK, WIDTH), BF),
        slot=((8, TOK), I32),
        start=((8, 128), I32),
        asked=((DEV, 1, 128), I32),
        asks=((DEV, 1, 128), I32),
        want_v=((SLOTS, 128), I32),
        rows_out=((2 * SLOTS, WIDTH // 2), BF),
        rows_in=((2 * SLOTS, WIDTH // 2), BF),
        grads_out=((2 * SLOTS, WIDTH // 2), BF),
        grads_in=((2 * SLOTS, WIDTH // 2), BF),
        count_out=((8, 128), F32),
        count_in=((NB, 8, 128), F32),
        slope_v=((TOK, 4 * HD), F32),
        gate_v=((TOK, HD), BF),
        kv_out=((HEADS, TOK, 2 * DH), BF),
        q_out=((HEADS, TOK // 2, 2 * DH), BF),
        kv_in=((SPAN, HEADS, TOK, 2 * DH), BF),
        q_in=((HEADS, TOK // 2, 2 * DH), BF),
        q_v=((2 * HEADS * TOK, 2 * DH), BF),
        qt_v=((DH, HEADS * TOK), BF),
        begin_v=((HEADS * TOK, 128), I32),
        w_v=((SPAN, HEADS * HEADS, TOK, TOK), BF),
        s_v=((SPAN, HEADS * HEADS, TOK, TOK), BF),
        att_v=((HEADS * TOK, 2 * DH), F32),
        att_out=((HEADS, TOK // 2, 2 * DH), ATT),
        att_in=((HEADS, TOK // 2, 2 * DH), ATT),
        d_out=((HEADS, TOK // 2, 2 * DH), BF),
        d_in=((HEADS, TOK // 2, 2 * DH), BF),
        dt_v=((DH, HEADS * TOK), BF),
        dq_v=((HEADS * TOK, 2 * DH), F32),
        dq_out=((HEADS, TOK // 2, 2 * DH), BF),
        dq_in=((HEADS, TOK // 2, 2 * DH), BF),
        g_out=((SPAN, HEADS, TOK, 2 * DH), BF),
        g_in=((SPAN, HEADS, TOK, 2 * DH), BF),
        joined=((TOK, 4 * HD), BF),
    )
    for name, width in (("early", WIDTH), ("late", 3 * HD)):
        scratch |= {
            name + "_part": ((WIDTH, width), BF),
            name + "_core": ((TOK, width), BF),
            name + "_held": ((TOK, width), BF),
            name + "_first": ((2, HEADS, 64, width // 2), BF),
            name + "_second": ((2, HEADS, 16, width // 2), BF),
            name + "_last": ((2, HEADS, 16, width // 2), BF),
            name + "_full": ((WIDTH, width), BF),
        }
    sems = dict(
        sems=(8,), load_sems=(4,), count_send=(NB,), count_recv=(NB,),
        kv_send=(SPAN, HEADS), kv_recv=(SPAN, HEADS), q_send=(HEADS,), q_recv=(HEADS,),
        a_send=(HEADS,), a_recv=(HEADS,), d_send=(HEADS,), d_recv=(HEADS,),
        g_send=(SPAN, HEADS), g_recv=(SPAN, HEADS), e_send=(HEADS,), e_recv=(HEADS,),
        red_send=(2, 5, 2, HEADS), red_recv=(2, 5, 2, HEADS), twin_send=(2, 2), twin_recv=(2, 2),
    )
    names = ["owner", "row", "seg", "table_hbm", "w_in_hbm", "w_out_hbm", "cot_hbm"]
    names += [*outs, *scratch, *sems]
    return pl.pallas_call(
        functools.partial(whole_kernel, names),
        out_shape=tuple(jax.ShapeDtypeStruct(*kind) for kind in outs.values()),
        in_specs=[VMEM] * 3 + [ANY] * 4,
        out_specs=(VMEM,) * len(outs),
        scratch_shapes=[pltpu.VMEM(*kind) for kind in scratch.values()]
        + [dma(shape) for shape in sems.values()],
        compiler_params=pltpu.CompilerParams(
            collective_id=0, has_side_effects=True, vmem_limit_bytes=58 << 20
        ),
        name="whole_layer",
    )(owner, row, seg, table, w_in, w_out, cot)


def scatter_kernel(want_ref, landed_ref, early_ref, late_ref, table_ref, w_in_ref, w_out_ref):
    part = table_ref.shape[0]
    rows = iota((part, SLOTS), 0) + pl.program_id(0) * part
    table_ref[...] = dot(hot(want_ref[:1, :] == rows), landed_ref[...])
    size = w_in_ref.shape[0]
    here = tile(pl.program_id(0), size)
    w_in_ref[:, :HD] = early_ref[here, :HD].astype(F32)
    w_in_ref[:, HD:] = late_ref[here, :].astype(F32)
    size = w_out_ref.shape[0]
    step = pl.program_id(0)
    w_out_ref[:, : WIDTH // 2] = early_ref[tile(step, size), HD:].astype(F32)
    below = pl.ds(pl.multiple_of(step * size + HD, size), size)
    w_out_ref[:, WIDTH // 2 :] = early_ref[below, HD:].astype(F32)


def scatter_add(want, landed, early, late):
    steps = 8
    still = lambda i: (0, 0)
    return pl.pallas_call(
        scatter_kernel,
        grid=(steps,),
        out_shape=(
            jax.ShapeDtypeStruct((ROWS, WIDTH), F32),
            jax.ShapeDtypeStruct((WIDTH, 4 * HD), F32),
            jax.ShapeDtypeStruct((HD, WIDTH), F32),
        ),
        in_specs=[
            pl.BlockSpec((8, SLOTS), still),
            pl.BlockSpec((SLOTS, WIDTH), still),
            pl.BlockSpec((WIDTH, WIDTH), still),
            pl.BlockSpec((WIDTH, 3 * HD), still),
        ],
        out_specs=(
            pl.BlockSpec((ROWS // steps, WIDTH), lambda i: (i, 0)),
            pl.BlockSpec((WIDTH // steps, 4 * HD), lambda i: (i, 0)),
            pl.BlockSpec((HD // steps, WIDTH), lambda i: (i, 0)),
        ),
        compiler_params=pltpu.CompilerParams(vmem_limit_bytes=32 << 20),
        name="scatter_rows",
    )(want, landed, early, late)


def per_device(table, item_owner, item_row, segment, w_in, w_out, cotangent):
    layer_out, want, landed, early, late = whole(
        item_owner[0], item_row, segment, table, w_in, w_out, cotangent[0]
    )
    table_grad, w_in_grad, w_out_grad = scatter_add(want, landed, early, late)
    return (layer_out[None], table_grad, w_in_grad, w_out_grad)


def solution(mesh):
    placed = (
        P(("bal", "grp"), None),
        P("grp", "bal", None),
        P("grp", "bal"),
        P("grp", "bal"),
        P(),
        P(),
        P("grp", "bal", None),
    )
    return jax.shard_map(
        per_device,
        mesh=mesh,
        in_specs=placed,
        out_specs=(P("grp", "bal", None), P(("bal", "grp"), None), P(), P()),
        check_vma=False,
    )
```

```python
import functools
import types

import jax
import jax.numpy as jnp
from jax import lax
from jax.experimental import pallas as pl
from jax.experimental.pallas import tpu as pltpu
from jax.sharding import PartitionSpec as P

MESH = pl.DeviceIdType.MESH
BF = jnp.bfloat16
F32 = jnp.float32
TOK = 256
WIDTH = 512
CAP = 8
ROWS = 2048
NB = 16
NG = 8
DEV = NB * NG
SLOTS = DEV * CAP


def iota(shape, dim):
    return lax.broadcasted_iota(jnp.int32, shape, dim)


def hot(mask):
    return jnp.where(mask, 1.0, 0.0).astype(BF)


def dot(a, b):
    return jnp.dot(a, b, preferred_element_type=F32)


def dot_t(a, b):
    return lax.dot_general(a, b, (((1,), (1,)), ((), ())), preferred_element_type=F32)


def column_of(line):
    size = line.shape[1]
    eye = iota((size, size), 0) == iota((size, size), 1)
    return jnp.sum(jnp.where(eye, line, 0.0), axis=1, keepdims=True)


def line_of(column):
    size = column.shape[0]
    eye = iota((size, size), 0) == iota((size, size), 1)
    return jnp.sum(jnp.where(eye, column, 0.0), axis=0, keepdims=True)


def place_of(z, x, y, rest):
    return lax.rem(z + x + y, 4) * 32 + rest


def device(p):
    rest = lax.rem(p, 32)
    x, y = rest // 8, lax.rem(rest, 8) // 2
    z = lax.rem(p // 32 + 8 - x - y, 4)
    return (z * 4 + x, lax.rem(rest, NG))


def greet_all(me):
    barrier = pltpu.get_barrier_semaphore()

    def greet(k, carry):
        pl.semaphore_signal(
            barrier, inc=1, device_id=device(lax.rem(me + k, DEV)), device_id_type=MESH
        )
        return carry

    lax.fori_loop(1, DEV, greet, 0)
    return barrier


def paired_halves(rows):
    count = rows.shape[0] // CAP
    split = rows.reshape(count, CAP, WIDTH)
    joined = jnp.concatenate([split[:, :, : WIDTH // 2], split[:, :, WIDTH // 2 :]], axis=1)
    return joined.reshape(count * 2 * CAP, WIDTH // 2).astype(BF)


def wait_bytes(view, sem):
    pltpu.make_async_copy(view, view, sem).wait()


HEADS = 4
DH = 64
HD = HEADS * DH
GROUP = TOK * NB
NORM_EPS = 1e-06
SPAN = 3
ATT = F32


def dot_rows(a, b):
    return lax.dot_general(a, b, (((0,), (0,)), ((), ())), preferred_element_type=F32)


def fold(rows):
    half = rows.shape[0] // 2
    return jnp.concatenate([rows[:half], rows[half:]], axis=1)


def unfold(rows):
    return jnp.concatenate([rows[:, :DH], rows[:, DH:]], axis=0)


def normalise(values):
    centred = values - jnp.mean(values, axis=-1, keepdims=True)
    scale = lax.rsqrt(jnp.mean(centred * centred, axis=-1, keepdims=True) + NORM_EPS)
    return centred * scale, scale


def norm_grad(grad, normed, scale):
    along = jnp.mean(grad * normed, axis=-1, keepdims=True)
    return scale * (grad - jnp.mean(grad, axis=-1, keepdims=True) - normed * along)


def tile(i, size=TOK):
    if isinstance(i, int):
        return pl.ds(i * size, size)
    return pl.ds(pl.multiple_of(i * size, size), size)


def fetch_rows(r, me, b, g, barrier):
    owner_line = r.owner[...]
    rest = lax.rem(owner_line, 32)
    owner_line = place_of(owner_line // 32, rest // 8, lax.rem(rest, 8) // 2, rest)
    owner_f = column_of(owner_line.astype(F32))
    owner = owner_f.astype(jnp.int32)
    lanes = iota((TOK, 128), 1)
    named = jnp.where(owner == lanes, 1.0, 0.0)
    before = hot(iota((TOK, TOK), 0) > iota((TOK, TOK), 1))
    rank = jnp.sum(dot(before, named.astype(BF)) * named, axis=1, keepdims=True)
    slot = owner_f * CAP + rank
    r.slot[...] = jnp.broadcast_to(line_of(slot), (8, TOK)).astype(jnp.int32)
    ask = column_of(r.row[...].astype(F32)) + 1.0
    high = jnp.floor(ask * (1.0 / 64.0))
    low = ask - 64.0 * high
    mine = rank.astype(jnp.int32) == lanes // 16
    named_t = hot(owner_line == iota((DEV, TOK), 0))
    r.asked[...] = (
        64.0 * dot(named_t, jnp.where(mine, high, 0.0).astype(BF))
        + dot(named_t, jnp.where(mine, low, 0.0).astype(BF))
    ).astype(jnp.int32).reshape(DEV, 1, 128)
    seg = column_of(r.seg[...].astype(F32)).astype(jnp.int32)
    below = jnp.sum(jnp.where(seg < lanes, 1.0, 0.0), axis=0, keepdims=True)
    r.count_out[...] = jnp.broadcast_to(below, (8, 128))
    r.count_in[b] = jnp.broadcast_to(below, (8, 128))
    own = pltpu.make_async_copy(r.asked.at[me], r.asks.at[me], r.sems.at[1])
    own.start()
    own.wait()
    pl.semaphore_wait(barrier, DEV - 1)

    def ask_for(k, carry):
        p = lax.rem(me + k, DEV)
        pltpu.make_async_remote_copy(
            src_ref=r.asked.at[p], dst_ref=r.asks.at[me], send_sem=r.sems.at[2],
            recv_sem=r.sems.at[3], device_id=device(p), device_id_type=MESH,
        ).start()
        return carry

    lax.fori_loop(1, DEV, ask_for, 0)
    tallies = []
    for k in range(1, NB):
        tally = pltpu.make_async_remote_copy(
            src_ref=r.count_out, dst_ref=r.count_in.at[b], send_sem=r.count_send.at[k],
            recv_sem=r.count_recv.at[k], device_id=(lax.rem(b + k, NB), g), device_id_type=MESH,
        )
        tally.start()
        tallies.append(tally)
    for k, (source, into) in enumerate(r.loads):
        pltpu.make_async_copy(source, into, r.load_sems.at[k]).wait()
    wait_bytes(r.asks.at[pl.ds(0, DEV - 1)], r.sems.at[3])
    got = r.asks[...].reshape(DEV, 128).astype(F32)
    got_high = jnp.floor(got * (1.0 / 64.0))
    got_low = got - 64.0 * got_high
    spread = hot(iota((SLOTS, DEV), 0) // CAP == iota((SLOTS, DEV), 1))
    every = 64.0 * dot(spread, got_high.astype(BF)) + dot(spread, got_low.astype(BF))
    pick = lax.rem(iota((SLOTS, 128), 0), CAP) * 16 == iota((SLOTS, 128), 1)
    want = jnp.sum(jnp.where(pick, every, 0.0), axis=1, keepdims=True) - 1.0
    want = jnp.broadcast_to(want, (SLOTS, 128))
    r.want_v[...] = want.astype(jnp.int32)

    def rows_of(first, count):
        rows = r.want_v[pl.ds(first, count), :]
        return dot(hot(rows[:, :1] == iota((count, ROWS), 1)), r.table_v[...])

    rows = RowExchange(
        me, rows_of, r.rows_out, r.rows_in, r.sems.at[4], r.sems.at[5], r.sems.at[1]
    )
    for i in range(4):
        rows.serve(i)
    r.want_t[...] = want.T[:8].astype(jnp.int32)
    pltpu.make_async_copy(r.want_t, r.want, r.store_sems.at[0]).start()
    for tally in tallies:
        tally.wait()
    total = jnp.sum(r.count_in[...], axis=0)
    r.start[...] = total.astype(jnp.int32)
    slot = slot.astype(jnp.int32)
    place = (slot // CAP) * 16 + lax.rem(slot, CAP)
    spots = iota((TOK, 2 * SLOTS), 1)
    left, right = hot(place == spots), hot(place + CAP == spots)
    rows.take()
    r.emb[:, : WIDTH // 2] = dot(left, r.rows_in[...]).astype(BF)
    r.emb[:, WIDTH // 2 :] = dot(right, r.rows_in[...]).astype(BF)
    return rows


class RowExchange:
    def __init__(self, me, rows_of, out, into, send, recv, local):
        self.me, self.rows_of, self.out, self.into = me, rows_of, out, into
        self.send, self.recv, self.local = send, recv, local

    def serve(self, i):
        me, part, peers = self.me, SLOTS // 4, DEV // 4
        c = lax.rem(me // peers + i, 4)
        found = paired_halves(self.rows_of(pl.multiple_of(c * part, part), part))
        self.out[pl.ds(pl.multiple_of(c * 2 * part, 2 * part), 2 * part), :] = found

        def give(k, carry):
            p = c * peers + lax.rem(me + k, peers)
            pltpu.make_async_remote_copy(
                src_ref=self.out.at[pl.ds(pl.multiple_of(p * 16, 16), 16)],
                dst_ref=self.into.at[pl.ds(pl.multiple_of(me * 16, 16), 16)],
                send_sem=self.send, recv_sem=self.recv,
                device_id=device(p), device_id_type=MESH,
            ).start()
            return carry

        lax.fori_loop(1 if i == 0 else 0, peers, give, 0)
        if i == 0:
            home = pl.ds(pl.multiple_of(me * 16, 16), 16)
            own = pltpu.make_async_copy(self.out.at[home], self.into.at[home], self.local)
            own.start()
            own.wait()

    def take(self):
        wait_bytes(self.into.at[pl.ds(0, 16 * (DEV - 1))], self.recv)

    def finish(self):
        wait_bytes(self.out.at[pl.ds(0, 16 * (DEV - 1))], self.send)


class Reduction:
    def __init__(self, r, name):
        for kind in ("part", "held", "first", "second", "third", "full", "send", "recv"):
            setattr(self, kind, getattr(r, name + "_" + kind))
        b, g = lax.axis_index("bal"), lax.axis_index("grp")
        z, x, y, c = b // 4, lax.rem(b, 4), g // 2, lax.rem(g, 2)
        by_y = (g, lambda p: (b, p))
        by_x = (x * 2 + c, lambda p: (z * 4 + p // 2, y * 2 + lax.rem(p, 2)))
        only_y = (y, lambda p: (b, p * 2 + c))
        only_x = (x, lambda p: (z * 4 + p, g))
        only_z = (z, lambda p: (p * 4 + x, g))
        self.groups = ((by_y, only_x, only_z), (by_x, only_y, only_z))

    def give(self, unit, phase, group, src, dst):
        here, device_of = group
        count = NG if phase in (0, 4) else 4
        for k in range(1, count):
            p = lax.rem(here + k, count)
            pltpu.make_async_remote_copy(
                src_ref=src(p), dst_ref=dst(here),
                send_sem=self.send.at[unit, phase], recv_sem=self.recv.at[unit, phase],
                device_id=device_of(p), device_id_type=MESH,
            ).start()

    def view(self, unit, phase):
        if phase == 0:
            return self.first.at[unit, pl.ds(0, NG - 1)]
        if phase == 4:
            return self.full.at[unit, pl.ds(0, (NG - 1) * 64)]
        if phase == 3:
            return self.full.at[unit, pl.ds(0, 3 * 16)]
        return (self.second if phase == 1 else self.third).at[unit, pl.ds(0, 3)]

    def step(self, number):
        for unit in (0, 1):
            if number > 0:
                wait_bytes(self.view(unit, number - 1), self.recv.at[unit, number - 1])
            self.step_of(number, unit)

    def step_of(self, number, unit):
        one, two, three = self.groups[unit]
        rows = pl.ds(pl.multiple_of(one[0] * 64, 64), 64)
        inner = pl.ds(pl.multiple_of(two[0] * 16, 16), 16)
        if number == 0:
            def piece(p):
                return self.part.at[unit, pl.ds(pl.multiple_of(p * 64, 64), 64)]

            self.give(unit, 0, one, piece, lambda p: self.first.at[unit, p])
            self.first[unit, one[0]] = self.part[unit, rows, :]
        elif number == 1:
            total = self.first[unit, 0].astype(F32)
            for p in range(1, NG):
                total += self.first[unit, p].astype(F32)
            self.held[unit] = total.astype(BF)

            def piece(p):
                return self.held.at[unit, pl.ds(pl.multiple_of(p * 16, 16), 16)]

            self.give(unit, 1, two, piece, lambda p: self.second.at[unit, p])
            self.second[unit, two[0]] = self.held[unit, inner, :]
        elif number == 2:
            total = self.second[unit, 0].astype(F32)
            for p in range(1, 4):
                total += self.second[unit, p].astype(F32)
            self.third[unit, three[0]] = total.astype(BF)
            mine = self.third.at[unit, three[0]]
            self.give(unit, 2, three, lambda p: mine, lambda p: self.third.at[unit, p])
        elif number == 3:
            total = self.third[unit, 0].astype(F32)
            for p in range(1, 4):
                total += self.third[unit, p].astype(F32)
            row = pl.multiple_of(one[0] * 64 + two[0] * 16, 16)
            self.full[unit, pl.ds(row, 16), :] = total.astype(BF)

            def line(p):
                at = pl.multiple_of(one[0] * 64 + p * 16, 16)
                return self.full.at[unit, pl.ds(at, 16)]

            self.give(unit, 3, two, lambda p: line(two[0]), line)
        elif number == 4:
            def block(p):
                return self.full.at[unit, pl.ds(pl.multiple_of(p * 64, 64), 64)]

            self.give(unit, 4, one, lambda p: block(one[0]), block)

    def finish(self):
        for unit in (0, 1):
            for phase in range(5):
                wait_bytes(self.view(unit, phase), self.send.at[unit, phase])


def whole_kernel(names, *refs):
    r = types.SimpleNamespace(**dict(zip(names, refs)))
    b, g = lax.axis_index("bal"), lax.axis_index("grp")
    me = place_of(b // 4, lax.rem(b, 4), g // 2, lax.rem(b, 4) * NG + g)
    barrier = greet_all(me)
    r.loads = (
        (r.table_hbm, r.table_v), (r.w_in_hbm, r.w_in), (r.w_out_hbm, r.w_out), (r.cot_hbm, r.cot),
    )
    for k, (source, into) in enumerate(r.loads):
        pltpu.make_async_copy(source, into, r.load_sems.at[k]).start()
    rows = fetch_rows(r, me, b, g, barrier)
    early = Reduction(r, "early")
    late = Reduction(r, "late")
    z, x = b // HEADS, lax.rem(b, HEADS)
    def remote(src, dst, send, recv, at_z, at_x):
        return pltpu.make_async_remote_copy(
            src_ref=src, dst_ref=dst, send_sem=send, recv_sem=recv,
            device_id=(at_z * HEADS + at_x, g), device_id_type=MESH,
        )

    def spread(out, into, send, recv):
        for h in range(HEADS):
            @pl.when(h != x)
            def _():
                remote(out.at[h], into.at[x], send.at[h], recv.at[x], z, h).start()

            @pl.when(h == x)
            def _():
                into[h] = out[h]

    def collect(out, into, send, recv):
        for h in range(HEADS):
            @pl.when(h != x)
            def _():
                remote(out.at[h], into.at[h], send.at[h], recv.at[h], z, h).wait_recv()

    def sent(out, into, send, recv):
        for h in range(HEADS):
            @pl.when(h != x)
            def _():
                remote(out.at[h], into.at[h], send.at[h], recv.at[h], z, h).wait_send()

    embedded = r.emb[...].astype(F32)
    normed, _ = normalise(embedded)
    normed = normed.astype(BF)
    pre = dot(normed, r.w_in[...])
    sig = jax.nn.sigmoid(pre)
    act = pre * sig
    r.gate_v[...] = act[:, :HD].astype(BF)
    for h in range(HEADS):
        value, query, key = (
            act[:, part * HD + h * DH : part * HD + (h + 1) * DH] for part in (1, 2, 3)
        )
        r.kv_out[h] = jnp.concatenate([key, value], axis=1).astype(BF)
        r.q_out[h] = fold(query * 0.5).astype(BF)
    spread(r.q_out, r.q_in, r.q_send, r.q_recv)
    for dz in range(SPAN):
        for h in range(HEADS):
            @pl.when((z + dz < HEADS) & ((h != x) | (dz > 0)))
            def _():
                remote(
                    r.kv_out.at[h], r.kv_in.at[dz, x], r.kv_send.at[dz, h], r.kv_recv.at[dz, x], z + dz, h
                ).start()

            if dz == 0:
                @pl.when(h == x)
                def _():
                    r.kv_in[0, h] = r.kv_out[h]

    r.slope_v[...] = sig * (1.0 + pre * (1.0 - sig))
    r.att_v[...] = jnp.zeros_like(r.att_v)
    r.dq_v[...] = jnp.zeros_like(r.dq_v)
    places = z * HEADS * TOK + iota((HEADS * TOK, 128), 0)
    starts = r.start[:1, :]
    begin = jnp.max(jnp.where(starts <= places, starts, 0).astype(F32), axis=1, keepdims=True)
    r.begin_v[...] = jnp.broadcast_to(begin, (HEADS * TOK, 128)).astype(jnp.int32)
    collect(r.q_out, r.q_in, r.q_send, r.q_recv)
    for h in range(HEADS):
        q = unfold(r.q_in[h].astype(F32))
        r.q_v[h * TOK : (h + 1) * TOK, :] = jnp.concatenate(
            [q, jnp.zeros((TOK, DH), F32)], axis=1
        ).astype(BF)
        r.qt_v[:, h * TOK : (h + 1) * TOK] = q.T.astype(BF)

    def forward_pair(dz, i, j):
        kv = r.kv_in[dz, j]
        scores = dot_t(r.q_v[tile(i), :], kv)
        half = jnp.tanh(scores)
        more = 1.0 + half
        first = ((z - dz) * HEADS + j) * TOK
        visible = iota((TOK, TOK), 1) >= r.begin_v[tile(i), :1] - first
        if dz == 0 and i == j:
            visible &= iota((TOK, TOK), 1) <= iota((TOK, TOK), 0)
        weight = jnp.where(visible, scores * more, 0.0).astype(BF)
        r.w_v[dz, i * HEADS + j] = weight
        r.s_v[dz, i * HEADS + j] = jnp.where(
            visible, more * (1.0 + scores * (1.0 - half)), 0.0
        ).astype(BF)
        return dot(weight, kv)

    def forward(dz, i):
        keys = range(HEADS) if dz == 1 else range(i + 1) if dz == 0 else range(i, HEADS)
        total = r.att_v[tile(i), :]
        for j in keys:
            total = total + forward_pair(dz, i, j)
        r.att_v[tile(i), :] = total

    def arrived(dz):
        for h in range(HEADS):
            def arrival():
                remote(
                    r.kv_out.at[h], r.kv_in.at[dz, h], r.kv_send.at[dz, h], r.kv_recv.at[dz, h], z, h
                ).wait_recv()

            if dz == 0:
                pl.when(h != x)(arrival)
            else:
                arrival()

    for dz in range(SPAN):
        @pl.when(z >= dz)
        def _():
            arrived(dz)
            if dz == 1:
                pl.loop(0, HEADS)(functools.partial(forward, dz))
            else:
                for i in range(HEADS):
                    forward(dz, i)

    for h in range(HEADS):
        att = r.att_v[h * TOK : (h + 1) * TOK, DH:] * (2.0 / GROUP)
        r.att_out[h] = fold(att).astype(ATT)
    spread(r.att_out, r.att_in, r.a_send, r.a_recv)
    cot = r.cot[...]
    d_mixed = dot_t(cot, r.w_out[...])
    gate = r.gate_v[...].astype(F32)
    collect(r.att_out, r.att_in, r.a_send, r.a_recv)

    attended = jnp.concatenate([unfold(r.att_in[h].astype(F32)) for h in range(HEADS)], axis=1)
    level, scale = normalise(attended)
    delta = norm_grad(d_mixed * gate, level, scale)
    for h in range(HEADS):
        r.d_out[h] = fold(delta[:, h * DH : (h + 1) * DH]).astype(BF)
    spread(r.d_out, r.d_in, r.d_send, r.d_recv)
    mixed = (level * gate).astype(BF)
    r.layer_v[...] = (dot(mixed, r.w_out[...]) + r.emb[...].astype(F32)).astype(BF)
    pltpu.make_async_copy(r.layer_v, r.layer_out, r.store_sems.at[1]).start()
    d_gate = (d_mixed * level).astype(BF).astype(F32)
    r.joined[:, :HD] = (d_gate * r.slope_v[:, :HD]).astype(BF)
    embedded = r.emb[...].astype(F32)
    normed = normalise(embedded)[0].astype(BF)
    r.early_part[0] = dot_rows(normed, r.joined[:, :HD]).astype(BF)
    out_grad = dot_rows(mixed, cot)
    r.early_part[1, :HD] = out_grad[:, : WIDTH // 2].astype(BF)
    r.early_part[1, HD:] = out_grad[:, WIDTH // 2 :].astype(BF)
    early.step(0)
    collect(r.d_out, r.d_in, r.d_send, r.d_recv)
    for h in range(HEADS):
        d = unfold(r.d_in[h].astype(F32))
        r.q_v[HEADS * TOK + h * TOK : HEADS * TOK + (h + 1) * TOK, :] = jnp.concatenate(
            [jnp.zeros((TOK, DH), F32), d], axis=1
        ).astype(BF)
        r.dt_v[:, h * TOK : (h + 1) * TOK] = d.T.astype(BF)

    def backward(dz):
        def keys(j):
            kv = r.kv_in[dz, j]

            queries = range(HEADS) if dz == 1 else range(j, HEADS) if dz == 0 else range(j + 1)
            dk = dv = jnp.zeros((DH, TOK), F32)
            for i in queries:
                product = dot_t(r.q_v[tile(HEADS + i), :], kv)
                d_score = (product * r.s_v[dz, i * HEADS + j].astype(F32)).astype(BF)
                r.dq_v[tile(i), :] += dot(d_score, kv)
                dk = dk + dot(r.qt_v[:, tile(i)], d_score)
                dv = dv + dot(r.dt_v[:, tile(i)], r.w_v[dz, i * HEADS + j])
            grads = jnp.concatenate([dk, dv], axis=0) * (2.0 / GROUP)
            r.g_out[dz, j] = grads.T.astype(BF)
            if dz == 0:
                @pl.when(j != x)
                def _():
                    remote(
                        r.g_out.at[0, j], r.g_in.at[0, x], r.g_send.at[0, j], r.g_recv.at[0, x], z, j
                    ).start()

                @pl.when(j == x)
                def _():
                    r.g_in[0, j] = r.g_out[0, j]
            else:
                remote(
                    r.g_out.at[dz, j], r.g_in.at[dz, x], r.g_send.at[dz, j], r.g_recv.at[dz, x], z - dz, j
                ).start()

        if dz == 1:
            pl.loop(0, HEADS)(keys)
        else:
            for j in range(HEADS):
                keys(j)

    for dz in reversed(range(SPAN)):
        @pl.when(z >= dz)
        def _():
            backward(dz)

        early.step(SPAN - dz)

    for h in range(HEADS):
        r.dq_out[h] = fold(r.dq_v[h * TOK : (h + 1) * TOK, :DH] * (1.0 / GROUP)).astype(BF)
    spread(r.dq_out, r.dq_in, r.e_send, r.e_recv)

    spread_in, spread_scale = normalise(embedded)
    normed = spread_in.astype(BF)
    for dz in reversed(range(SPAN)):
        for h in range(HEADS):
            def arrival():
                remote(
                    r.g_out.at[dz, h], r.g_in.at[dz, h], r.g_send.at[dz, h], r.g_recv.at[dz, h], z, h
                ).wait_recv()

            if dz == 0:
                pl.when(h != x)(arrival)
            else:
                pl.when(z + dz < HEADS)(arrival)

    collect(r.dq_out, r.dq_in, r.e_send, r.e_recv)
    for h in range(HEADS):
        total = r.g_in[0, h].astype(F32)
        for dz in range(1, SPAN):
            total += jnp.where(z + dz < HEADS, r.g_in[dz, h].astype(F32), 0.0)
        r.joined[:, HD + h * DH : HD + (h + 1) * DH] = total[:, DH:].astype(BF)
        r.joined[:, 2 * HD + h * DH : 2 * HD + (h + 1) * DH] = unfold(
            r.dq_in[h].astype(F32)
        ).astype(BF)
        r.joined[:, 3 * HD + h * DH : 3 * HD + (h + 1) * DH] = total[:, :DH].astype(BF)
    r.joined[:, HD:] = (r.joined[:, HD:].astype(F32) * r.slope_v[:, HD:]).astype(BF)
    for unit in (0, 1):
        first = HD + unit * 3 * HD // 2
        block = r.joined[:, first : first + 3 * HD // 2]
        r.late_part[unit] = dot_rows(normed, block).astype(BF)
    late.step(0)
    early.step(4)
    d_normed = dot_t(r.joined[...], r.w_in[...])
    r.demb[...] = (
        norm_grad(d_normed, spread_in, spread_scale) + r.cot[...].astype(F32)
    ).astype(BF)

    def grads_of(first, count):
        return dot(hot(r.slot[:1, :] == iota((count, TOK), 0) + first), r.demb[...])

    grads = RowExchange(
        me, grads_of, r.grads_out, r.grads_in, r.sems.at[6], r.sems.at[7], r.sems.at[1]
    )
    for i in range(4):
        grads.serve(i)
        late.step(i + 1)
    early.step(5)
    pltpu.make_async_copy(r.early_full, r.early, r.store_sems.at[2]).start()
    late.step(5)
    pltpu.make_async_copy(r.late_full, r.late, r.store_sems.at[3]).start()
    grads.take()
    halves = r.grads_in[...].astype(F32).reshape(DEV, 2 * CAP, WIDTH // 2)
    gathered = jnp.concatenate([halves[:, :CAP], halves[:, CAP:]], axis=2)
    r.landed_v[...] = gathered.reshape(SLOTS, WIDTH).astype(BF)
    pltpu.make_async_copy(r.landed_v, r.landed, r.store_sems.at[4]).start()

    sent(r.q_out, r.q_in, r.q_send, r.q_recv)
    sent(r.att_out, r.att_in, r.a_send, r.a_recv)
    sent(r.d_out, r.d_in, r.d_send, r.d_recv)
    sent(r.dq_out, r.dq_in, r.e_send, r.e_recv)
    for dz in range(SPAN):
        for h in range(HEADS):
            @pl.when((z + dz < HEADS) & ((h != x) | (dz > 0)))
            def _():
                remote(
                    r.kv_out.at[h], r.kv_in.at[dz, h], r.kv_send.at[dz, h], r.kv_recv.at[dz, h], z, h
                ).wait_send()

            @pl.when((z >= dz) & ((h != x) | (dz > 0)))
            def _():
                remote(
                    r.g_out.at[dz, h], r.g_in.at[dz, h], r.g_send.at[dz, h], r.g_recv.at[dz, h], z, h
                ).wait_send()
    early.finish()
    late.finish()
    wait_bytes(r.asked.at[pl.ds(0, DEV - 1)], r.sems.at[2])
    rows.finish()
    grads.finish()
    wait_bytes(r.want_t, r.store_sems.at[0])
    wait_bytes(r.layer_v, r.store_sems.at[1])
    wait_bytes(r.early_full, r.store_sems.at[2])
    wait_bytes(r.late_full, r.store_sems.at[3])
    wait_bytes(r.landed_v, r.store_sems.at[4])


VMEM = pl.BlockSpec(memory_space=pltpu.VMEM)
ANY = pl.BlockSpec(memory_space=pl.ANY)


def whole(owner, row, seg, table, w_in, w_out, cot):
    dma = pltpu.SemaphoreType.DMA
    I32 = jnp.int32
    outs = dict(
        layer_out=((TOK, WIDTH), BF),
        want=((8, SLOTS), I32),
        landed=((SLOTS, WIDTH), BF),
        early=((2, WIDTH, HD), BF),
        late=((2, WIDTH, 3 * HD // 2), BF),
    )
    scratch = dict(
        table_v=((ROWS, WIDTH), BF),
        w_in=((WIDTH, 4 * HD), BF),
        w_out=((HD, WIDTH), BF),
        cot=((TOK, WIDTH), BF),
        emb=((TOK, WIDTH), BF),
        demb=((TOK, WIDTH), BF),
        slot=((8, TOK), I32),
        start=((8, 128), I32),
        asked=((DEV, 1, 128), I32),
        asks=((DEV, 1, 128), I32),
        want_v=((SLOTS, 128), I32),
        rows_out=((2 * SLOTS, WIDTH // 2), BF),
        rows_in=((2 * SLOTS, WIDTH // 2), BF),
        grads_out=((2 * SLOTS, WIDTH // 2), BF),
        grads_in=((2 * SLOTS, WIDTH // 2), BF),
        count_out=((8, 128), F32),
        count_in=((NB, 8, 128), F32),
        slope_v=((TOK, 4 * HD), F32),
        gate_v=((TOK, HD), BF),
        kv_out=((HEADS, TOK, 2 * DH), BF),
        q_out=((HEADS, TOK // 2, 2 * DH), BF),
        kv_in=((SPAN, HEADS, TOK, 2 * DH), BF),
        q_in=((HEADS, TOK // 2, 2 * DH), BF),
        q_v=((2 * HEADS * TOK, 2 * DH), BF),
        qt_v=((DH, HEADS * TOK), BF),
        begin_v=((HEADS * TOK, 128), I32),
        w_v=((SPAN, HEADS * HEADS, TOK, TOK), BF),
        s_v=((SPAN, HEADS * HEADS, TOK, TOK), BF),
        att_v=((HEADS * TOK, 2 * DH), F32),
        att_out=((HEADS, TOK // 2, 2 * DH), ATT),
        att_in=((HEADS, TOK // 2, 2 * DH), ATT),
        d_out=((HEADS, TOK // 2, 2 * DH), BF),
        d_in=((HEADS, TOK // 2, 2 * DH), BF),
        dt_v=((DH, HEADS * TOK), BF),
        dq_v=((HEADS * TOK, 2 * DH), F32),
        dq_out=((HEADS, TOK // 2, 2 * DH), BF),
        dq_in=((HEADS, TOK // 2, 2 * DH), BF),
        g_out=((SPAN, HEADS, TOK, 2 * DH), BF),
        g_in=((SPAN, HEADS, TOK, 2 * DH), BF),
        joined=((TOK, 4 * HD), BF),
        want_t=((8, SLOTS), I32),
        layer_v=((TOK, WIDTH), BF),
        landed_v=((SLOTS, WIDTH), BF),
    )
    for name, width in (("early", HD), ("late", 3 * HD // 2)):
        scratch |= {
            name + "_part": ((2, WIDTH, width), BF),
            name + "_held": ((2, 64, width), BF),
            name + "_first": ((2, NG, 64, width), BF),
            name + "_second": ((2, 4, 16, width), BF),
            name + "_third": ((2, 4, 16, width), BF),
            name + "_full": ((2, WIDTH, width), BF),
        }
    sems = dict(
        sems=(8,), load_sems=(4,), count_send=(NB,), count_recv=(NB,),
        kv_send=(SPAN, HEADS), kv_recv=(SPAN, HEADS), q_send=(HEADS,), q_recv=(HEADS,),
        a_send=(HEADS,), a_recv=(HEADS,), d_send=(HEADS,), d_recv=(HEADS,),
        g_send=(SPAN, HEADS), g_recv=(SPAN, HEADS), e_send=(HEADS,), e_recv=(HEADS,),
        early_send=(2, 5), early_recv=(2, 5), late_send=(2, 5), late_recv=(2, 5),
        store_sems=(5,),
    )
    names = ["owner", "row", "seg", "table_hbm", "w_in_hbm", "w_out_hbm", "cot_hbm"]
    names += [*outs, *scratch, *sems]
    return pl.pallas_call(
        functools.partial(whole_kernel, names),
        out_shape=tuple(jax.ShapeDtypeStruct(*kind) for kind in outs.values()),
        in_specs=[VMEM] * 3 + [ANY] * 4,
        out_specs=(ANY,) * len(outs),
        scratch_shapes=[pltpu.VMEM(*kind) for kind in scratch.values()]
        + [dma(shape) for shape in sems.values()],
        compiler_params=pltpu.CompilerParams(
            collective_id=0, has_side_effects=True, vmem_limit_bytes=58 << 20
        ),
        name="whole_layer",
    )(owner, row, seg, table, w_in, w_out, cot)


def finish_kernel(
    want_hbm, landed_hbm, early_hbm, late_hbm, layer_hbm,
    table_out, w_in_out, w_out_out, layer_out,
    want, landed, early, late, layer, table, w_in, w_out, load, store,
):
    pairs = [(want_hbm, want)]
    quarter = SLOTS // 4
    for k in range(4):
        rows = pl.ds(k * quarter, quarter)
        pairs.append((landed_hbm.at[rows], landed.at[rows]))
    for k in (0, 1):
        pairs.append((early_hbm.at[k], early.at[k]))
    for k in (0, 1):
        pairs.append((late_hbm.at[k], late.at[k]))
    pairs.append((layer_hbm, layer))
    loads = [pltpu.make_async_copy(*pair, load.at[k]) for k, pair in enumerate(pairs)]
    for copy in loads:
        copy.start()
    stores = []

    def put(source, into, rows):
        copy = pltpu.make_async_copy(
            source.at[rows], into.at[rows], store.at[len(stores)]
        )
        copy.start()
        stores.append(copy)

    for copy in loads[:5]:
        copy.wait()
    part = ROWS // 4
    for i in range(4):
        rows = pl.ds(i * part, part)
        chosen = hot(want[:1, :] == iota((part, SLOTS), 0) + i * part)
        table[rows, :] = dot(chosen, landed[...])
        for k in (0, 1):
            put(table, table_out, pl.ds(i * part + k * part // 2, part // 2))
        if i == 0:
            for copy in loads[5:]:
                copy.wait()
            w_in[:, :HD] = early[0].astype(F32)
            for k in (0, 1):
                left = HD + k * 3 * HD // 2
                w_in[:, left : left + 3 * HD // 2] = late[k].astype(F32)
            w_out[:, : WIDTH // 2] = early[1, :HD].astype(F32)
            w_out[:, WIDTH // 2 :] = early[1, HD:].astype(F32)
            for k in range(4):
                put(w_in, w_in_out, pl.ds(k * 128, 128))
            put(w_out, w_out_out, pl.ds(0, HD))
            put(layer, layer_out, pl.ds(0, TOK))
    for copy in stores:
        copy.wait()


def finish(*operands):
    results = (
        jax.ShapeDtypeStruct((ROWS, WIDTH), F32),
        jax.ShapeDtypeStruct((WIDTH, 4 * HD), F32),
        jax.ShapeDtypeStruct((HD, WIDTH), F32),
        jax.ShapeDtypeStruct((TOK, WIDTH), BF),
    )
    return pl.pallas_call(
        finish_kernel,
        out_shape=results,
        in_specs=[ANY] * 5,
        out_specs=(ANY,) * 4,
        scratch_shapes=[pltpu.VMEM(operand.shape, operand.dtype) for operand in operands]
        + [pltpu.VMEM(kind.shape, kind.dtype) for kind in results[:3]]
        + [pltpu.SemaphoreType.DMA((10,)), pltpu.SemaphoreType.DMA((14,))],
        compiler_params=pltpu.CompilerParams(vmem_limit_bytes=58 << 20),
        name="finish",
    )(*operands)


def per_device(table, item_owner, item_row, segment, w_in, w_out, cotangent):
    layer_out, want, landed, early, late = whole(
        item_owner.reshape(1, TOK), item_row, segment, table, w_in, w_out, cotangent[0]
    )
    table_grad, w_in_grad, w_out_grad, layer_out = finish(
        want, landed, early, late, layer_out
    )
    return (layer_out[None], table_grad, w_in_grad, w_out_grad)


def solution(mesh):
    placed = (
        P(("bal", "grp"), None),
        P("grp", "bal", None),
        P("grp", "bal"),
        P("grp", "bal"),
        P(),
        P(),
        P("grp", "bal", None),
    )
    return jax.shard_map(
        per_device,
        mesh=mesh,
        in_specs=placed,
        out_specs=(P("grp", "bal", None), P(("bal", "grp"), None), P(), P()),
        check_vma=False,
    )
```
